512 devices in a mesh: ex: 32 (over z, core), fsdp: 16 (over y, x).
Axes of the slice: x: 4, y: 4, z: 16, core: 2. Of those that a mesh axis runs over, the one named last changes fastest.
Arguments:
- train_inputs: bfloat16 [512, 128, 5120], P(('ex', 'fsdp')), may hold values from -6 to 6
- train_upstream: bfloat16 [512, 128, 5120], P(('ex', 'fsdp')), may hold values from -6 to 6
- held_inputs: bfloat16 [128, 128, 5120], P('ex', 'fsdp'), may hold values from -6 to 6
- held_upstream: bfloat16 [128, 128, 5120], P('ex', 'fsdp'), may hold values from -6 to 6
- adapter_down: bfloat16 [5120, 128], P('fsdp'), may hold values from -0.078125 to 0.078125
- adapter_up: bfloat16 [128, 5120], P(None, 'fsdp'), may hold values from -0.5 to 0.5
- rank_signs_up: bfloat16 [128, 64], replicated, may hold values from -1 to 1, as said below
- rank_signs_down: bfloat16 [128, 64], replicated, may hold values from -1 to 1, as said below
- width_signs_up: bfloat16 [5120, 64], P('fsdp'), may hold values from -1 to 1, as said below
- width_signs_down: bfloat16 [5120, 64], P('fsdp'), may hold values from -1 to 1, as said below
Outputs:
- train_features: bfloat16 [512, 8192], P(('ex', 'fsdp'))
- influence: float32 [512, 128], P(('ex', 'fsdp'))
The draws below stay inside these ranges and needn't reach their ends.
Inputs may be any that keep to these rules, and one draw needn't show every extreme that they name: `rank_signs_up`: every entry is +1 or -1. `rank_signs_down`: every entry is +1 or -1. `width_signs_up`: every entry is +1 or -1. `width_signs_down`: every entry is +1 or -1.
All inputs are finite; a program needn't handle non-finite values.
Results may differ from the reference program's by a relative error of at most 0.0033.
Values may be sent and summed in bfloat16 or wider, within the bound.
No kernel may reach another device: no remote copies, remote signals or barrier semaphores. Data moves between devices by JAX's collectives and lax.ppermute only.
A program may use at most 64 MiB of HBM per device.

```python
import jax
import jax.numpy as jnp
from jax import lax

D = 5120
RANK = 128
K1 = 64
K2 = 64
SEQ = 128
TRAIN = 512
VAL = 128


def sign_table(key, rows, cols):
    return (2 * jax.random.randint(key, (rows, cols), 0, 2) - 1).astype(jnp.float32)


def draw_rank_signs_up(key, part):
    key = jax.random.fold_in(key, 11)
    return sign_table(key, RANK, K1).astype(jnp.bfloat16)


def draw_rank_signs_down(key, part):
    key = jax.random.fold_in(key, 23)
    return sign_table(key, RANK, K1).astype(jnp.bfloat16)


def draw_width_signs_up(key, part):
    key = jax.random.fold_in(key, 37)
    return sign_table(key, D, K2).astype(jnp.bfloat16)


def draw_width_signs_down(key, part):
    key = jax.random.fold_in(key, 41)
    return sign_table(key, D, K2).astype(jnp.bfloat16)


def shard_levels(own_key, dims, split, least, top_value):
    def one(position, shards_of):
        steps = jax.random.uniform(jax.random.fold_in(jax.random.fold_in(own_key, 6), position), (shards_of,), jnp.float32, least / len(split), top_value / len(split))
        return jnp.repeat(jnp.exp(steps), dims[position] // shards_of).reshape((-1,) + (1,) * (len(dims) - position - 1))

    factor_of = one(*split[0])
    for cut in split[1:]:
        factor_of = factor_of * one(*cut)
    return factor_of


def scatter_about(stream_key, extent, spread, most, shards=(), kind=jnp.bfloat16):
    gain = shard_levels(stream_key, extent, shards, -0.22, 0.18) if shards else 1.0
    result = jax.random.normal(stream_key, extent, jnp.float32) * spread * gain
    return jnp.minimum(jnp.maximum(result, -most), most).astype(kind)


def setup_inputs(seed: int = 0) -> dict:
    seeds = jax.random.split(jax.random.key(seed), 11)
    return {
        "train_inputs": scatter_about(seeds[0], (TRAIN, SEQ, D), 1.0, 6.0, ((0, 512),)),
        "train_upstream": scatter_about(seeds[1], (TRAIN, SEQ, D), 1.0, 6.0, ((0, 512),)),
        "held_inputs": scatter_about(seeds[2], (VAL, SEQ, D), 1.0, 6.0, ((0, 32), (1, 16))),
        "held_upstream": scatter_about(seeds[3], (VAL, SEQ, D), 1.0, 6.0, ((0, 32), (1, 16))),
        "adapter_down": scatter_about(seeds[4], (D, RANK), D ** -0.5, 0.078125, ((0, 16),)),
        "adapter_up": scatter_about(seeds[5], (RANK, D), RANK ** -0.5, 0.5, ((1, 16),)),
        "rank_signs_up": draw_rank_signs_up(jax.random.fold_in(seeds[10], 71), 0),
        "rank_signs_down": draw_rank_signs_down(jax.random.fold_in(seeds[10], 71), 0),
        "width_signs_up": draw_width_signs_up(jax.random.fold_in(seeds[10], 71), 0),
        "width_signs_down": draw_width_signs_down(jax.random.fold_in(seeds[10], 71), 0),
    }


EPSILON = 1e-06
HIGH = lax.Precision.HIGHEST

def features(inputs, upstream, map_up, map_down, wide_up, wide_down):

    def single(pair):
        inputs_one = pair[0].astype(jnp.float32)
        upstream_one = pair[1].astype(jnp.float32)
        left_up = jnp.dot(inputs_one, map_up, precision=HIGH)
        right_up = jnp.dot(upstream_one, wide_up, precision=HIGH)
        left_down = jnp.dot(upstream_one, map_down, precision=HIGH)
        right_down = jnp.dot(inputs_one, wide_down, precision=HIGH)
        block_up = jnp.dot(left_up.T, right_up, precision=HIGH)
        block_down = jnp.dot(left_down.T, right_down, precision=HIGH)
        return jnp.concatenate([block_up.reshape(-1), block_down.reshape(-1)])
    return lax.map(single, (inputs, upstream))

def scaled(values):
    return values * lax.rsqrt(lax.optimization_barrier(jnp.mean(values * values, axis=1, keepdims=True)) + EPSILON)

def reference(train_inputs, train_upstream, held_inputs, held_upstream, adapter_down, adapter_up, rank_signs_up, rank_signs_down, width_signs_up, width_signs_down):
    map_up = jnp.dot(adapter_down.astype(jnp.float32), rank_signs_up.astype(jnp.float32), precision=HIGH)
    map_down = jnp.dot(adapter_up.astype(jnp.float32).T, rank_signs_down.astype(jnp.float32), precision=HIGH)
    wide_up = width_signs_up.astype(jnp.float32)
    wide_down = width_signs_down.astype(jnp.float32)
    train_proj = features(train_inputs, train_upstream, map_up, map_down, wide_up, wide_down)
    held_proj = features(held_inputs, held_upstream, map_up, map_down, wide_up, wide_down)
    train_features = scaled(train_proj).astype(jnp.bfloat16)
    held_features = scaled(held_proj).astype(jnp.bfloat16)
    influence = jnp.dot(train_features, held_features.T, preferred_element_type=jnp.float32) / jnp.sqrt(jnp.float32(train_features.shape[1]))
    return (train_features, influence)
```

```python
import functools
import math

import jax
import jax.numpy as jnp
from jax import lax
from jax.experimental import pallas as pl
from jax.experimental.pallas import tpu as pltpu
from jax.sharding import Mesh, PartitionSpec as P

EPSILON = 1e-06
HIGH = lax.Precision.HIGHEST
PLANE = ("c", "y", "x")
EXTRA = 16
LIFT = 14.0
PRODUCTS = 40
COST = 20_000_000_000


def nt(a, b, precision=None):
    return lax.dot_general(
        a, b, (((1,), (1,)), ((), ())), precision=precision, preferred_element_type=jnp.float32
    )


def tn(a, b, precision=None):
    return lax.dot_general(
        a, b, (((0,), (0,)), ((), ())), precision=precision, preferred_element_type=jnp.float32
    )


def nn(a, b, precision=None):
    return lax.dot_general(
        a, b, (((1,), (0,)), ((), ())), precision=precision, preferred_element_type=jnp.float32
    )


def prepare_kernel(
    core_ref, down_ref, up_ref, rank_down_ref, rank_up_ref, wide_up_ref, wide_down_ref,
    xt_ref, gt_ref, xh_ref, gh_ref, block_ref, send_ref, adapter, rank, wide, sems,
):
    first = core_ref[0] == 0
    tokens = xt_ref.shape[0]
    held = xh_ref.shape[0]

    def copies(of_adapter, of_rank, of_wide, of_t, of_h):
        return [
            pltpu.make_async_copy(of_adapter, adapter, sems.at[0]),
            pltpu.make_async_copy(of_rank, rank, sems.at[1]),
            pltpu.make_async_copy(of_wide, wide, sems.at[2]),
            pltpu.make_async_copy(of_t, send_ref.at[pl.ds(0, tokens)], sems.at[3]),
            pltpu.make_async_copy(of_h, send_ref.at[pl.ds(tokens, held)], sems.at[4]),
        ]

    of_g = copies(up_ref, rank_down_ref, wide_up_ref, xt_ref, xh_ref)
    of_x = copies(down_ref, rank_up_ref, wide_down_ref, gt_ref, gh_ref)

    @pl.when(first)
    def _():
        for one in of_g:
            one.start()

    @pl.when(jnp.logical_not(first))
    def _():
        for one in of_x:
            one.start()

    for one in of_g[:3]:
        one.wait()
    rows = adapter.shape[0]
    half = rank.shape[0]
    blank = jnp.zeros(rank.shape, rank.dtype)
    mine = rank[...]
    folded = nt(
        adapter[...],
        jnp.concatenate([jnp.where(first, blank, mine), jnp.where(first, mine, blank)], axis=0),
    )
    signs = wide[...].astype(jnp.float32)
    blank = jnp.zeros_like(signs)
    signs = jnp.concatenate([jnp.where(first, signs, blank), jnp.where(first, blank, signs)], axis=0)
    top = jnp.max(jnp.abs(folded), axis=0, keepdims=True)
    exponent = jnp.floor(jnp.log2(jnp.maximum(top, 2.0**-100)))
    lane = lax.broadcasted_iota(jnp.int32, (1, 2 * half), 1)
    is_folded = (lane >= half) == first
    exponent = jnp.where(is_folded, exponent, LIFT)
    block_ref[pl.ds(0, rows), :] = folded * jnp.exp2(LIFT - exponent) + signs.T
    block_ref[pl.ds(rows, EXTRA), :] = jnp.broadcast_to(exponent, (EXTRA, 2 * half))
    for one in of_g[3:]:
        one.wait()


def decode_kernel(values_ref, factor_ref):
    chunks, tall, both = values_ref.shape
    local = tall - EXTRA
    for f in range(chunks):
        scale = jnp.exp2(values_ref[f, pl.ds(local, 1), :] - LIFT)
        value = values_ref[f, pl.ds(0, local), :] * scale
        high = value.astype(jnp.bfloat16)
        factor_ref[pl.ds(f * local, local), pl.ds(0, both)] = high
        low = value - high.astype(jnp.float32)
        factor_ref[pl.ds(f * local, local), pl.ds(both, both)] = low.astype(jnp.bfloat16)


def product_kernel(
    core_ref, factor_ref, xt_ref, gt_ref, xh_ref, gh_ref, recv_ref,
    own_ref, other_ref, held_ref, rows_ref, sems,
):
    first = core_ref[0] == 0
    tokens, width = xt_ref.shape
    held = xh_ref.shape[0]
    both = own_ref.shape[1]

    def copies(of_t, of_h):
        return [
            pltpu.make_async_copy(of_t, rows_ref.at[pl.ds(0, tokens)], sems.at[0]),
            pltpu.make_async_copy(of_h, rows_ref.at[pl.ds(2 * tokens, held)], sems.at[1]),
        ]

    of_x, of_g = copies(xt_ref, xh_ref), copies(gt_ref, gh_ref)
    of_recv = [
        pltpu.make_async_copy(
            recv_ref.at[pl.ds(0, tokens)], rows_ref.at[pl.ds(tokens, tokens)], sems.at[2]
        ),
        pltpu.make_async_copy(
            recv_ref.at[pl.ds(tokens, held)], rows_ref.at[pl.ds(2 * tokens + held, held)], sems.at[3]
        ),
    ]

    @pl.when(first)
    def _():
        for one in of_g:
            one.start()

    @pl.when(jnp.logical_not(first))
    def _():
        for one in of_x:
            one.start()

    for one in of_recv:
        one.start()
    for one in of_g + of_recv:
        one.wait()
    out = nn(rows_ref[...], factor_ref[...])
    out = out[:, :both] + out[:, both:]
    own_ref[...] = out[:tokens]
    other_ref[...] = out[tokens : 2 * tokens]
    own = out[2 * tokens : 2 * tokens + held]
    other = out[2 * tokens + held :]
    held_ref[pl.ds(0, held), :] = jnp.where(first, own, other)
    held_ref[pl.ds(held, held), :] = jnp.where(first, other, own)


def joined(product, half):
    lane = lax.broadcasted_iota(jnp.int32, (half, 2 * half), 1)
    return jnp.where(lane < half, product[:half], product[half:])


def scale_of(values):
    return lax.rsqrt(jnp.sum(values * values, keepdims=True) * (1.0 / values.size) + EPSILON)


def feature_kernel(core_ref, own_ref, recv_ref, held_ref, features_ref, out_ref, *, share, copies):
    first = core_ref[0] == 0
    own, recv = own_ref[...], recv_ref[...]
    of_g = jnp.where(first, own, recv)
    of_x = jnp.where(first, recv, own)
    product = tn(of_x, of_g, HIGH)
    turned = tn(of_g, of_x, HIGH)
    half = product.shape[0] // 2
    values = joined(product, half)
    scale = scale_of(values)
    features_ref[0] = (product * scale)[:half, :half].astype(jnp.bfloat16)
    features_ref[1] = (turned * scale)[half:, half:].astype(jnp.bfloat16)
    rounded = (values * scale).astype(jnp.bfloat16)
    rows = half // copies
    for i in range(out_ref.shape[0]):
        v, j = divmod(i, copies)
        value = held_ref[pl.ds(v * share, share), :]
        high = value.astype(jnp.bfloat16).astype(jnp.float32)
        pair = jnp.concatenate([high, value - high], axis=0).astype(jnp.bfloat16)
        out_ref[i, pl.ds(0, 2 * share), :] = pair
        out_ref[i, pl.ds(2 * share, rows), :] = rounded[j * rows : (j + 1) * rows]


def normal_kernel(part_ref, tokens_ref, out_ref, held_ref, *, share):
    count = tokens_ref.shape[0] // 2
    both = tokens_ref.shape[2]
    pairs = tokens_ref[:, pl.ds(0, 2 * share), :].astype(jnp.float32)
    tokens = (pairs[:, :share] + pairs[:, share:]).reshape(2 * count * share, both)
    product = tn(tokens[count * share :], tokens[: count * share], HIGH)
    half = both // 2
    values = joined(product, half)
    held_ref[...] = values * scale_of(values)
    rows = out_ref.shape[1]
    start = pl.multiple_of(part_ref[0] * rows, rows)
    own = held_ref[pl.ds(start, rows), :].astype(jnp.bfloat16)
    for i in range(out_ref.shape[0]):
        out_ref[i] = own


def influence_kernel(slot_ref, tokens_ref, held_ref, out_ref, *, share, slots):
    mates, _, both = tokens_ref.shape
    rows = tokens_ref.shape[1] - 2 * share
    train = tokens_ref[:, pl.ds(2 * share, rows), :].reshape(mates * rows, both)
    every = nt(train, held_ref[...])
    n, m = every.shape
    r = lax.broadcasted_iota(jnp.int32, (n, m), 0)
    q = lax.broadcasted_iota(jnp.int32, (n, m), 1)
    every = jnp.where(lax.rem(r, rows) == lax.rem(q, rows), every, 0.0)
    trains = n // rows
    summed = jnp.sum(every.reshape(trains, rows // 8, 8, m), axis=1).reshape(trains * 8, m)
    row = lax.broadcasted_iota(jnp.int32, (m, out_ref.shape[1]), 0)
    col = lax.broadcasted_iota(jnp.int32, (m, out_ref.shape[1]), 1)
    place = jnp.where(col == lax.div(row, rows) * slots + slot_ref[0], 1.0, 0.0)
    out_ref[...] = nn(summed, place, HIGH)


SMEM = pl.BlockSpec(memory_space=pltpu.SMEM)
VMEM = pl.BlockSpec(memory_space=pltpu.VMEM)
HBM = pl.BlockSpec(memory_space=pl.ANY)


def shape(dims, dtype=jnp.float32):
    return jax.ShapeDtypeStruct(dims, dtype)


def params(mib):
    return pltpu.CompilerParams(vmem_limit_bytes=mib << 20)


def shards(
    train_inputs, train_upstream, held_inputs, held_upstream, adapter_down, adapter_up,
    rank_signs_up, rank_signs_down, width_signs_up, width_signs_down, *, sizes,
):
    nz, nc, ny, nx = sizes
    mates = nc * ny * nx
    core = lax.axis_index("c").astype(jnp.int32).reshape(1)
    part = lax.axis_index("x").astype(jnp.int32).reshape(1)
    slot = (lax.axis_index("c") * ny + lax.axis_index("y")).astype(jnp.int32).reshape(1)
    tokens, width = train_inputs.shape[1:]
    groups, share = held_inputs.shape[:2]
    held_rows = groups * share
    local, rank = adapter_down.shape
    half = rank_signs_up.shape[1]
    both = 2 * half
    rows = half // nx
    bf16 = jnp.bfloat16
    tall = local + EXTRA
    every_rows = 2 * (tokens + held_rows)

    sequences = (
        train_inputs.reshape(tokens, width), train_upstream.reshape(tokens, width),
        held_inputs.reshape(held_rows, width), held_upstream.reshape(held_rows, width),
    )
    block, send = pl.pallas_call(
        prepare_kernel,
        out_shape=(shape((tall, both)), shape((tokens + held_rows, width), bf16)),
        in_specs=[SMEM] + [HBM] * 10,
        out_specs=(VMEM, VMEM),
        scratch_shapes=[
            pltpu.VMEM((local, rank), bf16),
            pltpu.VMEM((half, rank), bf16),
            pltpu.VMEM((half, local), bf16),
            pltpu.SemaphoreType.DMA((5,)),
        ],
        compiler_params=params(60),
        name="prepare",
    )(
        core, adapter_down, adapter_up.T, rank_signs_down.T, rank_signs_up.T,
        width_signs_up.T, width_signs_down.T, *sequences,
    )
    blocks = jnp.broadcast_to(block.astype(jnp.float16), (ny * nx, tall, both))
    gathered = lax.all_to_all(blocks, ("y", "x"), 0, 0)
    swap = [(0, 1), (1, 0)]
    recv = lax.ppermute(send, "c", swap)

    factor = pl.pallas_call(
        decode_kernel,
        out_shape=shape((width, 2 * both), bf16),
        in_specs=[VMEM],
        out_specs=VMEM,
        compiler_params=params(16),
        cost_estimate=pl.CostEstimate(flops=COST, bytes_accessed=8 * width * both, transcendentals=0),
        name="decode",
    )(gathered.astype(jnp.float32))
    own, other, held_products = pl.pallas_call(
        product_kernel,
        out_shape=(shape((tokens, both)), shape((tokens, both)), shape((2 * held_rows, both))),
        in_specs=[SMEM, VMEM] + [HBM] * 5,
        out_specs=(VMEM, VMEM, VMEM),
        scratch_shapes=[
            pltpu.VMEM((every_rows, width), bf16),
            pltpu.SemaphoreType.DMA((4,)),
        ],
        compiler_params=params(PRODUCTS),
        name="products",
    )(core, factor, *sequences, recv)
    swapped = lax.ppermute(other, "c", swap)

    features, to_plane = pl.pallas_call(
        functools.partial(feature_kernel, share=share, copies=nx),
        out_shape=(shape((2, half, half), bf16), shape((mates, 2 * share + rows, both), bf16)),
        in_specs=[SMEM, VMEM, VMEM, VMEM],
        out_specs=(VMEM, VMEM),
        compiler_params=params(40),
        name="train_features",
    )(core, own, swapped, held_products)
    in_plane = lax.all_to_all(to_plane, PLANE, 0, 0)

    to_z = pl.pallas_call(
        functools.partial(normal_kernel, share=share),
        out_shape=shape((nz, rows, both), bf16),
        in_specs=[SMEM, VMEM],
        out_specs=VMEM,
        scratch_shapes=[pltpu.VMEM((half, both), jnp.float32)],
        compiler_params=params(16),
        name="held_features",
    )(part, in_plane)
    held_every = lax.all_to_all(to_z, "z", 0, 0)

    partial = pl.pallas_call(
        functools.partial(influence_kernel, share=share, slots=nc * ny),
        out_shape=shape((mates * 8, nz * nc * ny)),
        in_specs=[SMEM, VMEM, VMEM],
        out_specs=VMEM,
        compiler_params=params(16),
        name="partial_influence",
    )(slot, in_plane, held_every.reshape(nz * rows, both))
    back = lax.all_to_all(partial.reshape(mates, 8, nz * nc * ny), PLANE, 0, 0)
    influence = jnp.sum(back, axis=(0, 1)).reshape(1, -1) * (1.0 / math.sqrt(half * both))
    return features.reshape(1, half * both), influence


def solution(mesh):
    ex, fsdp = mesh.devices.shape
    ny = nx = math.isqrt(fsdp)
    sizes = (ex // 2, 2, ny, nx)
    fine = Mesh(mesh.devices.reshape(sizes), ("z", "c", "y", "x"))
    e, f = ("z", "c"), ("y", "x")
    every = ("z", "c", "y", "x")
    placed = (
        P(every, None, None), P(every, None, None), P(e, f, None), P(e, f, None),
        P(f, None), P(None, f), P(), P(), P(f, None), P(f, None),
    )
    return jax.shard_map(
        functools.partial(shards, sizes=sizes),
        mesh=fine,
        in_specs=placed,
        out_specs=(P(every, None), P(every, None)),
        check_vma=False,
    )
```

```python
import functools
import math

import jax
import jax.numpy as jnp
from jax import lax
from jax.experimental import pallas as pl
from jax.experimental.pallas import tpu as pltpu
from jax.sharding import Mesh, PartitionSpec as P

EPSILON = 1e-06
HIGH = lax.Precision.HIGHEST
PLANE = ("c", "y", "x")
EXTRA = 8
LIFT = 14.0
COST = 20_000_000_000


def nt(a, b, precision=None):
    return lax.dot_general(
        a, b, (((1,), (1,)), ((), ())), precision=precision, preferred_element_type=jnp.float32
    )


def tn(a, b, precision=None):
    return lax.dot_general(
        a, b, (((0,), (0,)), ((), ())), precision=precision, preferred_element_type=jnp.float32
    )


def nn(a, b, precision=None):
    return lax.dot_general(
        a, b, (((1,), (0,)), ((), ())), precision=precision, preferred_element_type=jnp.float32
    )


def prepare_kernel(
    core_ref, down_ref, up_ref, rank_down_ref, rank_up_ref, wide_up_ref, wide_down_ref,
    block_ref, adapter, rank, wide, sems,
):
    first = core_ref[0] == 0

    def copies(of_adapter, of_rank, of_wide):
        return [
            pltpu.make_async_copy(of_adapter, adapter, sems.at[0]),
            pltpu.make_async_copy(of_rank, rank, sems.at[1]),
            pltpu.make_async_copy(of_wide, wide, sems.at[2]),
        ]

    of_g = copies(up_ref, rank_down_ref, wide_up_ref)
    of_x = copies(down_ref, rank_up_ref, wide_down_ref)

    @pl.when(first)
    def _():
        for one in of_g:
            one.start()

    @pl.when(jnp.logical_not(first))
    def _():
        for one in of_x:
            one.start()

    for one in of_g:
        one.wait()
    rows = adapter.shape[0]
    half = rank.shape[0]
    blank = jnp.zeros(rank.shape, rank.dtype)
    mine = rank[...]
    folded = nt(
        adapter[...],
        jnp.concatenate([jnp.where(first, blank, mine), jnp.where(first, mine, blank)], axis=0),
    )
    signs = wide[...].astype(jnp.float32)
    blank = jnp.zeros_like(signs)
    signs = jnp.concatenate([jnp.where(first, signs, blank), jnp.where(first, blank, signs)], axis=0)
    top = jnp.max(jnp.abs(folded), axis=0, keepdims=True)
    exponent = jnp.floor(jnp.log2(jnp.maximum(top, 2.0**-100)))
    lane = lax.broadcasted_iota(jnp.int32, (1, 2 * half), 1)
    is_folded = (lane >= half) == first
    exponent = jnp.where(is_folded, exponent, LIFT)
    block_ref[pl.ds(0, rows), :] = folded * jnp.exp2(LIFT - exponent) + signs.T
    block_ref[pl.ds(rows, EXTRA), :] = jnp.broadcast_to(exponent, (EXTRA, 2 * half))


def pick_kernel(core_ref, xt_ref, gt_ref, xh_ref, gh_ref, keep_ref, send_ref, sems):
    first = core_ref[0] == 0
    tokens = xt_ref.shape[0]
    held = xh_ref.shape[0]

    def copies(own_t, own_h, other_t, other_h):
        return [
            pltpu.make_async_copy(other_t, send_ref.at[pl.ds(0, tokens)], sems.at[0]),
            pltpu.make_async_copy(other_h, send_ref.at[pl.ds(tokens, held)], sems.at[1]),
            pltpu.make_async_copy(own_t, keep_ref.at[pl.ds(0, tokens)], sems.at[2]),
            pltpu.make_async_copy(own_h, keep_ref.at[pl.ds(tokens, held)], sems.at[3]),
        ]

    of_g = copies(gt_ref, gh_ref, xt_ref, xh_ref)
    of_x = copies(xt_ref, xh_ref, gt_ref, gh_ref)

    @pl.when(first)
    def _():
        for one in of_g:
            one.start()

    @pl.when(jnp.logical_not(first))
    def _():
        for one in of_x:
            one.start()

    for one in of_g:
        one.wait()


def decode_kernel(values_ref, factor_ref):
    chunks, tall, both = values_ref.shape
    local = tall - EXTRA
    for f in range(chunks):
        scale = jnp.exp2(values_ref[f, pl.ds(local, 1), :] - LIFT)
        value = values_ref[f, pl.ds(0, local), :] * scale
        high = value.astype(jnp.bfloat16)
        factor_ref[pl.ds(f * local, local), pl.ds(0, both)] = high
        low = value - high.astype(jnp.float32)
        factor_ref[pl.ds(f * local, local), pl.ds(both, both)] = low.astype(jnp.bfloat16)


def product_kernel(factor_ref, rows_ref, *refs):
    train_ref, held_ref = refs[-2:]
    tokens, both = train_ref.shape
    value = nn(rows_ref[...], factor_ref[...])
    value = value[:, :both] + value[:, both:]
    train_ref[...] = value[:tokens]
    held_ref[...] = value[tokens:]


def joined(product, half):
    lane = lax.broadcasted_iota(jnp.int32, (half, 2 * half), 1)
    return jnp.where(lane < half, product[:half], product[half:])


def scale_of(values):
    return lax.rsqrt(jnp.sum(values * values, keepdims=True) * (1.0 / values.size) + EPSILON)


def kinds(core_ref, own_ref, pair_ref):
    first = core_ref[0] == 0
    own = own_ref[...]
    return jnp.where(first, own, pair_ref[0]), jnp.where(first, pair_ref[1], own)


def spread_kernel(
    core_ref, own_ref, pair_ref, held_own_ref, held_other_ref, out_ref, scale_ref, *, share, copies
):
    of_g, of_x = kinds(core_ref, own_ref, pair_ref)
    product = tn(of_x, of_g, HIGH)
    half = product.shape[0] // 2
    values = joined(product, half)
    scale = scale_of(values)
    scale_ref[...] = jnp.broadcast_to(scale, scale_ref.shape)
    rounded = (values * scale).astype(jnp.bfloat16)
    rows = half // copies
    groups = out_ref.shape[0] // (2 * copies)
    first = core_ref[0] == 0
    own, other = held_own_ref[...], held_other_ref[...]
    for c, held in enumerate((jnp.where(first, own, other), jnp.where(first, other, own))):
        high = held.astype(jnp.bfloat16).astype(jnp.float32)
        low = held - high
        for v in range(groups):
            part = slice(v * share, (v + 1) * share)
            pair = jnp.concatenate([high[part], low[part]], axis=0).astype(jnp.bfloat16)
            for j in range(copies):
                i = (c * groups + v) * copies + j
                out_ref[i, pl.ds(0, 2 * share), :] = pair
                out_ref[i, pl.ds(2 * share, rows), :] = rounded[j * rows : (j + 1) * rows]


def feature_kernel(core_ref, own_ref, pair_ref, scale_ref, features_ref):
    of_g, of_x = kinds(core_ref, own_ref, pair_ref)
    half = features_ref.shape[1]
    scale = scale_ref[pl.ds(0, 1), :]
    features_ref[0] = (tn(of_x, of_g, HIGH) * scale)[:half, :half].astype(jnp.bfloat16)
    features_ref[1] = (tn(of_g, of_x, HIGH) * scale)[half:, half:].astype(jnp.bfloat16)


def normal_kernel(part_ref, tokens_ref, out_ref, held_ref, *, share):
    count = tokens_ref.shape[0] // 2
    both = tokens_ref.shape[2]
    pairs = tokens_ref[:, pl.ds(0, 2 * share), :].astype(jnp.float32)
    tokens = (pairs[:, :share] + pairs[:, share:]).reshape(2 * count * share, both)
    product = tn(tokens[count * share :], tokens[: count * share], HIGH)
    half = both // 2
    values = joined(product, half)
    held_ref[...] = values * scale_of(values)
    rows = out_ref.shape[1]
    start = pl.multiple_of(part_ref[0] * rows, rows)
    own = held_ref[pl.ds(start, rows), :].astype(jnp.bfloat16)
    for i in range(out_ref.shape[0]):
        out_ref[i] = own


def influence_kernel(slot_ref, tokens_ref, held_ref, out_ref, *, share, slots):
    mates, _, both = tokens_ref.shape
    rows = tokens_ref.shape[1] - 2 * share
    train = tokens_ref[:, pl.ds(2 * share, rows), :].reshape(mates * rows, both)
    every = nt(train, held_ref[...])
    n, m = every.shape
    r = lax.broadcasted_iota(jnp.int32, (n, m), 0)
    q = lax.broadcasted_iota(jnp.int32, (n, m), 1)
    every = jnp.where(lax.rem(r, rows) == lax.rem(q, rows), every, 0.0)
    trains = n // rows
    summed = jnp.sum(every.reshape(trains, rows // 8, 8, m), axis=1).reshape(trains * 8, m)
    row = lax.broadcasted_iota(jnp.int32, (m, out_ref.shape[1]), 0)
    col = lax.broadcasted_iota(jnp.int32, (m, out_ref.shape[1]), 1)
    place = jnp.where(col == lax.div(row, rows) * slots + slot_ref[0], 1.0, 0.0)
    out_ref[...] = nn(summed, place, HIGH)


SMEM = pl.BlockSpec(memory_space=pltpu.SMEM)
VMEM = pl.BlockSpec(memory_space=pltpu.VMEM)
HBM = pl.BlockSpec(memory_space=pl.ANY)


def shape(dims, dtype=jnp.float32):
    return jax.ShapeDtypeStruct(dims, dtype)


def params(mib):
    return pltpu.CompilerParams(vmem_limit_bytes=mib << 20)


def shards(
    train_inputs, train_upstream, held_inputs, held_upstream, adapter_down, adapter_up,
    rank_signs_up, rank_signs_down, width_signs_up, width_signs_down, *, sizes,
):
    nz, nc, ny, nx = sizes
    mates = nc * ny * nx
    core = lax.axis_index("c").astype(jnp.int32).reshape(1)
    part = lax.axis_index("x").astype(jnp.int32).reshape(1)
    slot = (lax.axis_index("c") * ny + lax.axis_index("y")).astype(jnp.int32).reshape(1)
    tokens, width = train_inputs.shape[1:]
    groups, share = held_inputs.shape[:2]
    held_rows = groups * share
    local, rank = adapter_down.shape
    half = rank_signs_up.shape[1]
    both = 2 * half
    rows = half // nx
    bf16 = jnp.bfloat16
    tall = local + EXTRA

    sequences = (
        train_inputs.reshape(tokens, width), train_upstream.reshape(tokens, width),
        held_inputs.reshape(held_rows, width), held_upstream.reshape(held_rows, width),
    )
    block = pl.pallas_call(
        prepare_kernel,
        out_shape=shape((tall, both)),
        in_specs=[SMEM] + [HBM] * 6,
        out_specs=VMEM,
        scratch_shapes=[
            pltpu.VMEM((local, rank), bf16),
            pltpu.VMEM((half, rank), bf16),
            pltpu.VMEM((half, local), bf16),
            pltpu.SemaphoreType.DMA((3,)),
        ],
        compiler_params=params(60),
        name="prepare",
    )(
        core, adapter_down, adapter_up.T, rank_signs_down.T, rank_signs_up.T,
        width_signs_up.T, width_signs_down.T,
    )
    blocks = jnp.broadcast_to(block.astype(jnp.float16), (ny * nx, tall, both))
    gathered = lax.all_to_all(blocks, ("y", "x"), 0, 0)
    keep, send = pl.pallas_call(
        pick_kernel,
        out_shape=(shape((tokens + held_rows, width), bf16),) * 2,
        in_specs=[SMEM] + [HBM] * 4,
        out_specs=(VMEM, VMEM),
        scratch_shapes=[pltpu.SemaphoreType.DMA((4,))],
        compiler_params=params(60),
        name="pick",
    )(core, *sequences)
    swap = [(0, 1), (1, 0)]
    recv = lax.ppermute(send, "c", swap)

    factor = pl.pallas_call(
        decode_kernel,
        out_shape=shape((width, 2 * both), bf16),
        in_specs=[VMEM],
        out_specs=VMEM,
        compiler_params=params(16),
        cost_estimate=pl.CostEstimate(flops=COST, bytes_accessed=8 * width * both, transcendentals=0),
        name="decode",
    )(gathered.astype(jnp.float32))
    def products(*operands):
        return pl.pallas_call(
            product_kernel,
            out_shape=(shape((tokens, both)), shape((held_rows, both))),
            in_specs=[VMEM] * len(operands),
            out_specs=(VMEM, VMEM),
            compiler_params=params(16),
            name="products",
        )(*operands)

    other, held_other = products(factor, recv)
    own, held_own = products(factor, keep, held_other)
    pair = lax.all_gather(other, "c")

    to_plane, scale = pl.pallas_call(
        functools.partial(spread_kernel, share=share, copies=nx),
        out_shape=(shape((mates, 2 * share + rows, both), bf16), shape((8, both))),
        in_specs=[SMEM] + [VMEM] * 4,
        out_specs=(VMEM, VMEM),
        compiler_params=params(40),
        name="spread",
    )(core, own, pair, held_own, held_other)
    features = pl.pallas_call(
        feature_kernel,
        out_shape=shape((2, half, half), bf16),
        in_specs=[SMEM] + [VMEM] * 3,
        out_specs=VMEM,
        compiler_params=params(16),
        name="train_features",
    )(core, own, pair, scale)
    in_plane = lax.all_to_all(to_plane, PLANE, 0, 0)

    to_z = pl.pallas_call(
        functools.partial(normal_kernel, share=share),
        out_shape=shape((nz, rows, both), bf16),
        in_specs=[SMEM, VMEM],
        out_specs=VMEM,
        scratch_shapes=[pltpu.VMEM((half, both), jnp.float32)],
        compiler_params=params(16),
        name="held_features",
    )(part, in_plane)
    held_every = lax.all_to_all(to_z, "z", 0, 0)

    partial = pl.pallas_call(
        functools.partial(influence_kernel, share=share, slots=nc * ny),
        out_shape=shape((mates * 8, nz * nc * ny)),
        in_specs=[SMEM, VMEM, VMEM],
        out_specs=VMEM,
        compiler_params=params(16),
        name="partial_influence",
    )(slot, in_plane, held_every.reshape(nz * rows, both))
    back = lax.all_to_all(partial.reshape(mates, 8, nz * nc * ny), PLANE, 0, 0)
    influence = jnp.sum(back, axis=(0, 1)).reshape(1, -1) * (1.0 / math.sqrt(half * both))
    return features.reshape(1, half * both), influence


def solution(mesh):
    ex, fsdp = mesh.devices.shape
    ny = nx = math.isqrt(fsdp)
    sizes = (ex // 2, 2, ny, nx)
    fine = Mesh(mesh.devices.reshape(sizes), ("z", "c", "y", "x"))
    e, f = ("z", "c"), ("y", "x")
    every = ("z", "c", "y", "x")
    placed = (
        P(every, None, None), P(every, None, None), P(e, f, None), P(e, f, None),
        P(f, None), P(None, f), P(), P(), P(f, None), P(f, None),
    )
    return jax.shard_map(
        functools.partial(shards, sizes=sizes),
        mesh=fine,
        in_specs=placed,
        out_specs=(P(every, None), P(every, None)),
        check_vma=False,
    )
```

```python
import functools
import math

import jax
import jax.numpy as jnp
from jax import lax
from jax.experimental import pallas as pl
from jax.experimental.pallas import tpu as pltpu
from jax.sharding import Mesh, PartitionSpec as P

EPSILON = 1e-06
HIGH = lax.Precision.HIGHEST
PLANE = ("y", "x", "c")
EXTRA = 8
LIFT = 14.0
COST = 20_000_000_000


def nt(a, b, precision=None):
    return lax.dot_general(
        a, b, (((1,), (1,)), ((), ())), precision=precision, preferred_element_type=jnp.float32
    )


def tn(a, b, precision=None):
    return lax.dot_general(
        a, b, (((0,), (0,)), ((), ())), precision=precision, preferred_element_type=jnp.float32
    )


def nn(a, b, precision=None):
    return lax.dot_general(
        a, b, (((1,), (0,)), ((), ())), precision=precision, preferred_element_type=jnp.float32
    )


def prepare_kernel(
    down_ref, up_ref, rank_down_ref, rank_up_ref, wide_up_ref, wide_down_ref,
    block_ref, adapter, rank, wide, sems,
):
    first = lax.axis_index("c") == 0

    def copies(of_adapter, of_rank, of_wide):
        return [
            pltpu.make_async_copy(of_adapter, adapter, sems.at[0]),
            pltpu.make_async_copy(of_rank, rank, sems.at[1]),
            pltpu.make_async_copy(of_wide, wide, sems.at[2]),
        ]

    of_g = copies(up_ref, rank_down_ref, wide_up_ref)
    of_x = copies(down_ref, rank_up_ref, wide_down_ref)

    @pl.when(first)
    def _():
        for one in of_g:
            one.start()

    @pl.when(jnp.logical_not(first))
    def _():
        for one in of_x:
            one.start()

    for one in of_g:
        one.wait()
    rows = adapter.shape[0]
    half = rank.shape[0]
    blank = jnp.zeros(rank.shape, rank.dtype)
    mine = rank[...]
    folded = nt(
        adapter[...],
        jnp.concatenate([jnp.where(first, blank, mine), jnp.where(first, mine, blank)], axis=0),
    )
    signs = wide[...].astype(jnp.float32)
    blank = jnp.zeros_like(signs)
    signs = jnp.concatenate([jnp.where(first, signs, blank), jnp.where(first, blank, signs)], axis=0)
    top = jnp.max(jnp.abs(folded), axis=0, keepdims=True)
    exponent = jnp.floor(jnp.log2(jnp.maximum(top, 2.0**-100)))
    lane = lax.broadcasted_iota(jnp.int32, (1, 2 * half), 1)
    is_folded = (lane >= half) == first
    exponent = jnp.where(is_folded, exponent, LIFT)
    block_ref[pl.ds(0, rows), :] = folded * jnp.exp2(LIFT - exponent) + signs.T
    block_ref[pl.ds(rows, EXTRA), :] = jnp.broadcast_to(exponent, (EXTRA, 2 * half))


def pick_kernel(core_ref, xt_ref, gt_ref, xh_ref, gh_ref, keep_ref, send_ref, sems):
    first = core_ref[0] == 0
    tokens = xt_ref.shape[0]
    held = xh_ref.shape[0]

    def copies(own_t, own_h, other_t, other_h):
        return [
            pltpu.make_async_copy(other_t, send_ref.at[pl.ds(0, tokens)], sems.at[0]),
            pltpu.make_async_copy(other_h, send_ref.at[pl.ds(tokens, held)], sems.at[1]),
            pltpu.make_async_copy(own_t, keep_ref.at[pl.ds(0, tokens)], sems.at[2]),
            pltpu.make_async_copy(own_h, keep_ref.at[pl.ds(tokens, held)], sems.at[3]),
        ]

    of_g = copies(gt_ref, gh_ref, xt_ref, xh_ref)
    of_x = copies(xt_ref, xh_ref, gt_ref, gh_ref)

    @pl.when(first)
    def _():
        for one in of_g:
            one.start()

    @pl.when(jnp.logical_not(first))
    def _():
        for one in of_x:
            one.start()

    for one in of_g:
        one.wait()


def decode_kernel(values_ref, factor_ref):
    chunks, tall, both = values_ref.shape
    local = tall - EXTRA
    for f in range(chunks):
        scale = jnp.exp2(values_ref[f, pl.ds(local, 1), :] - LIFT)
        value = values_ref[f, pl.ds(0, local), :] * scale
        high = value.astype(jnp.bfloat16)
        factor_ref[pl.ds(f * local, local), pl.ds(0, both)] = high
        low = value - high.astype(jnp.float32)
        factor_ref[pl.ds(f * local, local), pl.ds(both, both)] = low.astype(jnp.bfloat16)


def product_kernel(factor_ref, rows_ref, *refs):
    train_ref, held_ref = refs[-2:]
    tokens, both = train_ref.shape
    value = nn(rows_ref[...], factor_ref[...])
    value = value[:, :both] + value[:, both:]
    train_ref[...] = value[:tokens]
    held_ref[...] = value[tokens:]


def joined(product, half):
    lane = lax.broadcasted_iota(jnp.int32, (half, 2 * half), 1)
    return jnp.where(lane < half, product[:half], product[half:])


def scale_of(values):
    return lax.rsqrt(jnp.sum(values * values, keepdims=True) * (1.0 / values.size) + EPSILON)


def kinds(core_ref, own_ref, pair_ref):
    first = core_ref[0] == 0
    own = own_ref[...]
    return jnp.where(first, own, pair_ref[0]), jnp.where(first, pair_ref[1], own)


def spread_kernel(
    core_ref, own_ref, pair_ref, held_own_ref, held_other_ref, out_ref, scale_ref, *, share, copies
):
    of_g, of_x = kinds(core_ref, own_ref, pair_ref)
    product = tn(of_x, of_g, HIGH)
    half = product.shape[0] // 2
    values = joined(product, half)
    scale = scale_of(values)
    scale_ref[...] = jnp.broadcast_to(scale, scale_ref.shape)
    rounded = (values * scale).astype(jnp.bfloat16)
    rows = half // copies
    groups = out_ref.shape[0] // (2 * copies)
    first = core_ref[0] == 0
    own, other = held_own_ref[...], held_other_ref[...]
    for c, held in enumerate((jnp.where(first, own, other), jnp.where(first, other, own))):
        high = held.astype(jnp.bfloat16).astype(jnp.float32)
        low = held - high
        for v in range(groups):
            part = slice(v * share, (v + 1) * share)
            pair = jnp.concatenate([high[part], low[part]], axis=0).astype(jnp.bfloat16)
            for j in range(copies):
                i = (v * copies + j) * 2 + c
                out_ref[i, pl.ds(0, 2 * share), :] = pair
                out_ref[i, pl.ds(2 * share, rows), :] = rounded[j * rows : (j + 1) * rows]


def feature_kernel(core_ref, own_ref, pair_ref, scale_ref, features_ref):
    of_g, of_x = kinds(core_ref, own_ref, pair_ref)
    half = features_ref.shape[1]
    scale = scale_ref[pl.ds(0, 1), :]
    features_ref[0] = (tn(of_x, of_g, HIGH) * scale)[:half, :half].astype(jnp.bfloat16)
    features_ref[1] = (tn(of_g, of_x, HIGH) * scale)[half:, half:].astype(jnp.bfloat16)


def normal_kernel(part_ref, tokens_ref, out_ref, held_ref, *, share):
    count = tokens_ref.shape[0] // 2
    both = tokens_ref.shape[2]
    pairs = tokens_ref[:, pl.ds(0, 2 * share), :].astype(jnp.float32)
    tokens = (pairs[:, :share] + pairs[:, share:]).reshape(count, 2, share, both)
    of_g = tokens[:, 0].reshape(count * share, both)
    of_x = tokens[:, 1].reshape(count * share, both)
    product = tn(of_x, of_g, HIGH)
    half = both // 2
    values = joined(product, half)
    held_ref[...] = values * scale_of(values)
    rows = out_ref.shape[1]
    start = pl.multiple_of(part_ref[0] * rows, rows)
    own = held_ref[pl.ds(start, rows), :].astype(jnp.bfloat16)
    for i in range(out_ref.shape[0]):
        out_ref[i] = own


def influence_kernel(slot_ref, tokens_ref, held_ref, out_ref, *, share, slots):
    mates, _, both = tokens_ref.shape
    rows = tokens_ref.shape[1] - 2 * share
    train = tokens_ref[:, pl.ds(2 * share, rows), :].reshape(mates * rows, both)
    every = nt(train, held_ref[...])
    n, m = every.shape
    r = lax.broadcasted_iota(jnp.int32, (n, m), 0)
    q = lax.broadcasted_iota(jnp.int32, (n, m), 1)
    every = jnp.where(lax.rem(r, rows) == lax.rem(q, rows), every, 0.0)
    trains = n // rows
    summed = jnp.sum(every.reshape(trains, rows, m), axis=1)
    row = lax.broadcasted_iota(jnp.int32, (m, out_ref.shape[2]), 0)
    col = lax.broadcasted_iota(jnp.int32, (m, out_ref.shape[2]), 1)
    place = jnp.where(col == lax.div(row, rows) * slots + slot_ref[0], 1.0, 0.0)
    placed = nn(summed, place, HIGH)
    for i in range(trains):
        out_ref[i] = placed[i : i + 1]


SMEM = pl.BlockSpec(memory_space=pltpu.SMEM)
VMEM = pl.BlockSpec(memory_space=pltpu.VMEM)
HBM = pl.BlockSpec(memory_space=pl.ANY)


def shape(dims, dtype=jnp.float32):
    return jax.ShapeDtypeStruct(dims, dtype)


def params(mib):
    return pltpu.CompilerParams(vmem_limit_bytes=mib << 20)


def shards(
    train_inputs, train_upstream, held_inputs, held_upstream, adapter_down, adapter_up,
    rank_signs_up, rank_signs_down, width_signs_up, width_signs_down, *, sizes,
):
    nz, nc, ny, nx = sizes
    mates = nc * ny * nx
    core = lax.axis_index("c").astype(jnp.int32).reshape(1)
    part = lax.axis_index("x").astype(jnp.int32).reshape(1)
    slot = (lax.axis_index("c") * ny + lax.axis_index("y")).astype(jnp.int32).reshape(1)
    tokens, width = train_inputs.shape[1:]
    groups, share = held_inputs.shape[:2]
    held_rows = groups * share
    local, rank = adapter_down.shape
    half = rank_signs_up.shape[1]
    both = 2 * half
    rows = half // nx
    bf16 = jnp.bfloat16
    tall = local + EXTRA

    sequences = (
        train_inputs.reshape(tokens, width), train_upstream.reshape(tokens, width),
        held_inputs.reshape(held_rows, width), held_upstream.reshape(held_rows, width),
    )
    pin = lambda v: pltpu.with_memory_space_constraint(v, pltpu.HBM)
    block = pl.pallas_call(
        prepare_kernel,
        out_shape=shape((tall, both)),
        in_specs=[HBM] * 6,
        out_specs=VMEM,
        scratch_shapes=[
            pltpu.VMEM((local, rank), bf16),
            pltpu.VMEM((half, rank), bf16),
            pltpu.VMEM((half, local), bf16),
            pltpu.SemaphoreType.DMA((3,)),
        ],
        compiler_params=params(16),
        name="prepare",
    )(
        *map(pin, (
            adapter_down, adapter_up.T, rank_signs_down.T, rank_signs_up.T,
            width_signs_up.T, width_signs_down.T,
        ))
    )
    blocks = jnp.broadcast_to(block.astype(jnp.float16), (ny * nx, tall, both))
    gathered = lax.all_to_all(blocks, ("y", "x"), 0, 0)
    keep, send = pl.pallas_call(
        pick_kernel,
        out_shape=(shape((tokens + held_rows, width), bf16),) * 2,
        in_specs=[SMEM] + [HBM] * 4,
        out_specs=(VMEM, VMEM),
        scratch_shapes=[pltpu.SemaphoreType.DMA((4,))],
        compiler_params=params(60),
        name="pick",
    )(core, *map(pin, sequences))
    swap = [(0, 1), (1, 0)]
    recv = lax.ppermute(send, "c", swap)

    factor = pl.pallas_call(
        decode_kernel,
        out_shape=shape((width, 2 * both), bf16),
        in_specs=[VMEM],
        out_specs=VMEM,
        compiler_params=params(16),
        cost_estimate=pl.CostEstimate(flops=COST, bytes_accessed=8 * width * both, transcendentals=0),
        name="decode",
    )(gathered.astype(jnp.float32))
    def products(*operands):
        return pl.pallas_call(
            product_kernel,
            out_shape=(shape((tokens, both)), shape((held_rows, both))),
            in_specs=[VMEM] * len(operands),
            out_specs=(VMEM, VMEM),
            compiler_params=params(16),
            name="products",
        )(*operands)

    other, held_other = products(factor, recv)
    own, held_own = products(factor, keep, held_other)
    pair = lax.all_gather(other, "c")

    to_plane, scale = pl.pallas_call(
        functools.partial(spread_kernel, share=share, copies=nx),
        out_shape=(shape((mates, 2 * share + rows, both), bf16), shape((8, both))),
        in_specs=[SMEM] + [VMEM] * 4,
        out_specs=(VMEM, VMEM),
        compiler_params=params(40),
        name="spread",
    )(core, own, pair, held_own, held_other)
    features = pl.pallas_call(
        feature_kernel,
        out_shape=shape((2, half, half), bf16),
        in_specs=[SMEM] + [VMEM] * 3,
        out_specs=VMEM,
        compiler_params=params(16),
        name="train_features",
    )(core, own, pair, scale)
    in_plane = lax.all_to_all(to_plane, PLANE, 0, 0)

    to_z = pl.pallas_call(
        functools.partial(normal_kernel, share=share),
        out_shape=shape((nz, rows, both), bf16),
        in_specs=[SMEM, VMEM],
        out_specs=VMEM,
        scratch_shapes=[pltpu.VMEM((half, both), jnp.float32)],
        compiler_params=params(16),
        name="held_features",
    )(part, in_plane)
    held_every = lax.all_to_all(to_z, "z", 0, 0)

    partial = pl.pallas_call(
        functools.partial(influence_kernel, share=share, slots=nc * ny),
        out_shape=shape((mates, 1, nz * nc * ny)),
        in_specs=[SMEM, VMEM, VMEM],
        out_specs=VMEM,
        compiler_params=params(16),
        name="partial_influence",
    )(slot, in_plane, held_every.reshape(nz * rows, both))
    back = lax.all_to_all(partial, PLANE, 0, 0)
    influence = jnp.sum(back, axis=(0, 1)).reshape(1, -1) * (1.0 / math.sqrt(half * both))
    return features.reshape(1, half * both), influence


def solution(mesh):
    ex, fsdp = mesh.devices.shape
    ny = nx = math.isqrt(fsdp)
    sizes = (ex // 2, 2, ny, nx)
    fine = Mesh(mesh.devices.reshape(sizes), ("z", "c", "y", "x"))
    e, f = ("z", "c"), ("y", "x")
    every = ("z", "c", "y", "x")
    placed = (
        P(every, None, None), P(every, None, None), P(e, f, None), P(e, f, None),
        P(f, None), P(None, f), P(), P(), P(f, None), P(f, None),
    )
    return jax.shard_map(
        functools.partial(shards, sizes=sizes),
        mesh=fine,
        in_specs=placed,
        out_specs=(P(every, None), P(every, None)),
        check_vma=False,
    )
```

```python
import functools
import math

import jax
import jax.numpy as jnp
from jax import lax
from jax.experimental import pallas as pl
from jax.experimental.pallas import tpu as pltpu
from jax.sharding import Mesh, PartitionSpec as P

EPSILON = 1e-06
HIGH = lax.Precision.HIGHEST
PLANE = ("y", "x", "c")
EXTRA = 8
LIFT = 14.0
COST = 20_000_000_000


def nt(a, b, precision=None):
    return lax.dot_general(
        a, b, (((1,), (1,)), ((), ())), precision=precision, preferred_element_type=jnp.float32
    )


def tn(a, b, precision=None):
    return lax.dot_general(
        a, b, (((0,), (0,)), ((), ())), precision=precision, preferred_element_type=jnp.float32
    )


def nn(a, b, precision=None):
    return lax.dot_general(
        a, b, (((1,), (0,)), ((), ())), precision=precision, preferred_element_type=jnp.float32
    )


def prepare_kernel(
    down_ref, up_ref, rank_down_ref, rank_up_ref, wide_up_ref, wide_down_ref,
    block_ref, adapter, rank, wide, sems,
):
    first = lax.axis_index("c") == 0

    def copies(of_adapter, of_rank, of_wide):
        return [
            pltpu.make_async_copy(of_adapter, adapter, sems.at[0]),
            pltpu.make_async_copy(of_rank, rank, sems.at[1]),
            pltpu.make_async_copy(of_wide, wide, sems.at[2]),
        ]

    of_g = copies(up_ref, rank_down_ref, wide_up_ref)
    of_x = copies(down_ref, rank_up_ref, wide_down_ref)

    @pl.when(first)
    def _():
        for one in of_g:
            one.start()

    @pl.when(jnp.logical_not(first))
    def _():
        for one in of_x:
            one.start()

    for one in of_g:
        one.wait()
    rows = adapter.shape[0]
    half = rank.shape[0]
    blank = jnp.zeros(rank.shape, rank.dtype)
    mine = rank[...]
    folded = nt(
        adapter[...],
        jnp.concatenate([jnp.where(first, blank, mine), jnp.where(first, mine, blank)], axis=0),
    )
    signs = wide[...].astype(jnp.float32)
    blank = jnp.zeros_like(signs)
    signs = jnp.concatenate([jnp.where(first, signs, blank), jnp.where(first, blank, signs)], axis=0)
    top = jnp.max(jnp.abs(folded), axis=0, keepdims=True)
    exponent = jnp.floor(jnp.log2(jnp.maximum(top, 2.0**-100)))
    lane = lax.broadcasted_iota(jnp.int32, (1, 2 * half), 1)
    is_folded = (lane >= half) == first
    exponent = jnp.where(is_folded, exponent, LIFT)
    block_ref[pl.ds(0, rows), :] = folded * jnp.exp2(LIFT - exponent) + signs.T
    block_ref[pl.ds(rows, EXTRA), :] = jnp.broadcast_to(exponent, (EXTRA, 2 * half))


def pick_kernel(xt_ref, gt_ref, xh_ref, gh_ref, keep_ref, send_ref, sems):
    first = lax.axis_index("c") == 0
    tokens = xt_ref.shape[0]
    held = xh_ref.shape[0]

    def copies(own_t, own_h, other_t, other_h):
        return [
            pltpu.make_async_copy(other_t, send_ref.at[pl.ds(0, tokens)], sems.at[0]),
            pltpu.make_async_copy(other_h, send_ref.at[pl.ds(tokens, held)], sems.at[1]),
            pltpu.make_async_copy(own_t, keep_ref.at[pl.ds(0, tokens)], sems.at[2]),
            pltpu.make_async_copy(own_h, keep_ref.at[pl.ds(tokens, held)], sems.at[3]),
        ]

    of_g = copies(gt_ref, gh_ref, xt_ref, xh_ref)
    of_x = copies(xt_ref, xh_ref, gt_ref, gh_ref)

    @pl.when(first)
    def _():
        for one in of_g:
            one.start()

    @pl.when(jnp.logical_not(first))
    def _():
        for one in of_x:
            one.start()

    for one in of_g:
        one.wait()


def decode_kernel(values_ref, factor_ref):
    chunks, tall, both = values_ref.shape
    local = tall - EXTRA
    for f in range(chunks):
        scale = jnp.exp2(values_ref[f, pl.ds(local, 1), :] - LIFT)
        value = values_ref[f, pl.ds(0, local), :] * scale
        high = value.astype(jnp.bfloat16)
        factor_ref[pl.ds(f * local, local), pl.ds(0, both)] = high
        low = value - high.astype(jnp.float32)
        factor_ref[pl.ds(f * local, local), pl.ds(both, both)] = low.astype(jnp.bfloat16)


def product_kernel(factor_ref, rows_ref, *refs):
    train_ref, held_ref = refs[-2:]
    tokens, both = train_ref.shape
    value = nn(rows_ref[...], factor_ref[...])
    value = value[:, :both] + value[:, both:]
    train_ref[...] = value[:tokens]
    held_ref[...] = value[tokens:]


def halves(value):
    high = value.astype(jnp.bfloat16)
    return high, (value - high.astype(jnp.float32)).astype(jnp.bfloat16)


def stacked(a, b):
    a_high, a_low = halves(a)
    b_high, b_low = halves(b)
    return tn(
        jnp.concatenate([a_high, a_high, a_low], axis=0),
        jnp.concatenate([b_high, b_low, b_high], axis=0),
    )


def joined(product, half):
    lane = lax.broadcasted_iota(jnp.int32, (half, 2 * half), 1)
    return jnp.where(lane < half, product[:half], product[half:])


def scale_of(values):
    return lax.rsqrt(jnp.sum(values * values, keepdims=True) * (1.0 / values.size) + EPSILON)


def kinds(own_ref, pair_ref):
    first = lax.axis_index("c") == 0
    own = own_ref[...]
    return jnp.where(first, own, pair_ref[0]), jnp.where(first, pair_ref[1], own)


def spread_kernel(
    own_ref, pair_ref, held_own_ref, held_other_ref, out_ref, scale_ref, *, share, copies
):
    of_g, of_x = kinds(own_ref, pair_ref)
    product = stacked(of_x, of_g)
    half = product.shape[0] // 2
    values = joined(product, half)
    scale = scale_of(values)
    scale_ref[...] = jnp.broadcast_to(scale, scale_ref.shape)
    rounded = (values * scale).astype(jnp.bfloat16)
    rows = half // copies
    groups = out_ref.shape[0] // (2 * copies)
    first = lax.axis_index("c") == 0
    own, other = held_own_ref[...], held_other_ref[...]
    for c, held in enumerate((jnp.where(first, own, other), jnp.where(first, other, own))):
        high = held.astype(jnp.bfloat16).astype(jnp.float32)
        low = held - high
        for v in range(groups):
            part = slice(v * share, (v + 1) * share)
            pair = jnp.concatenate([high[part], low[part]], axis=0).astype(jnp.bfloat16)
            for j in range(copies):
                i = (v * copies + j) * 2 + c
                out_ref[i, pl.ds(0, 2 * share), :] = pair
                out_ref[i, pl.ds(2 * share, rows), :] = rounded[j * rows : (j + 1) * rows]


def feature_kernel(own_ref, pair_ref, scale_ref, features_ref):
    of_g, of_x = kinds(own_ref, pair_ref)
    half = features_ref.shape[1]
    scale = scale_ref[pl.ds(0, 1), :]
    features_ref[0] = (tn(of_x, of_g, HIGH) * scale)[:half, :half].astype(jnp.bfloat16)
    features_ref[1] = (tn(of_g, of_x, HIGH) * scale)[half:, half:].astype(jnp.bfloat16)


def normal_kernel(tokens_ref, out_ref, held_ref, *, share):
    count = tokens_ref.shape[0] // 2
    both = tokens_ref.shape[2]
    pairs = tokens_ref[:, pl.ds(0, 2 * share), :].astype(jnp.float32)
    tokens = (pairs[:, :share] + pairs[:, share:]).reshape(count, 2, share, both)
    of_g = tokens[:, 0].reshape(count * share, both)
    of_x = tokens[:, 1].reshape(count * share, both)
    product = stacked(of_x, of_g)
    half = both // 2
    values = joined(product, half)
    held_ref[...] = values * scale_of(values)
    rows = out_ref.shape[1]
    start = pl.multiple_of(lax.axis_index("x") * rows, rows)
    own = held_ref[pl.ds(start, rows), :].astype(jnp.bfloat16)
    for i in range(out_ref.shape[0]):
        out_ref[i] = own


def influence_kernel(tokens_ref, held_ref, out_ref, *, share, groups):
    slots = 2 * groups
    slot = lax.axis_index("c") * groups + lax.axis_index("y")
    mates, _, both = tokens_ref.shape
    rows = tokens_ref.shape[1] - 2 * share
    train = tokens_ref[:, pl.ds(2 * share, rows), :].reshape(mates * rows, both)
    every = nt(train, held_ref[...])
    n, m = every.shape
    r = lax.broadcasted_iota(jnp.int32, (n, m), 0)
    q = lax.broadcasted_iota(jnp.int32, (n, m), 1)
    every = jnp.where(lax.rem(r, rows) == lax.rem(q, rows), every, 0.0)
    trains = n // rows
    summed = jnp.sum(every.reshape(trains, rows, m), axis=1)
    row = lax.broadcasted_iota(jnp.int32, (m, out_ref.shape[2]), 0)
    col = lax.broadcasted_iota(jnp.int32, (m, out_ref.shape[2]), 1)
    place = jnp.where(col == lax.div(row, rows) * slots + slot, 1.0, 0.0)
    high = summed.astype(jnp.bfloat16).astype(jnp.float32)
    middle = (summed - high).astype(jnp.bfloat16).astype(jnp.float32)
    terms = jnp.concatenate([high, middle, summed - high - middle], axis=0)
    terms = nn(terms.astype(jnp.bfloat16), place.astype(jnp.bfloat16))
    placed = terms[:trains] + terms[trains : 2 * trains] + terms[2 * trains :]
    for i in range(trains):
        out_ref[i] = placed[i : i + 1]


VMEM = pl.BlockSpec(memory_space=pltpu.VMEM)
HBM = pl.BlockSpec(memory_space=pl.ANY)


def shape(dims, dtype=jnp.float32):
    return jax.ShapeDtypeStruct(dims, dtype)


def params(mib):
    return pltpu.CompilerParams(vmem_limit_bytes=mib << 20)


def shards(
    train_inputs, train_upstream, held_inputs, held_upstream, adapter_down, adapter_up,
    rank_signs_up, rank_signs_down, width_signs_up, width_signs_down, *, sizes,
):
    nz, nc, ny, nx = sizes
    mates = nc * ny * nx
    tokens, width = train_inputs.shape[1:]
    groups, share = held_inputs.shape[:2]
    held_rows = groups * share
    local, rank = adapter_down.shape
    half = rank_signs_up.shape[1]
    both = 2 * half
    rows = half // nx
    bf16 = jnp.bfloat16
    tall = local + EXTRA

    sequences = (
        train_inputs.reshape(tokens, width), train_upstream.reshape(tokens, width),
        held_inputs.reshape(held_rows, width), held_upstream.reshape(held_rows, width),
    )
    pin = lambda v: pltpu.with_memory_space_constraint(v, pltpu.HBM)
    block = pl.pallas_call(
        prepare_kernel,
        out_shape=shape((tall, both)),
        in_specs=[HBM] * 6,
        out_specs=VMEM,
        scratch_shapes=[
            pltpu.VMEM((local, rank), bf16),
            pltpu.VMEM((half, rank), bf16),
            pltpu.VMEM((half, local), bf16),
            pltpu.SemaphoreType.DMA((3,)),
        ],
        compiler_params=params(16),
        name="prepare",
    )(
        *map(pin, (
            adapter_down, adapter_up.T, rank_signs_down.T, rank_signs_up.T,
            width_signs_up.T, width_signs_down.T,
        ))
    )
    blocks = jnp.broadcast_to(block.astype(jnp.float16), (ny * nx, tall, both))
    gathered = lax.all_to_all(blocks, ("y", "x"), 0, 0)
    keep, send = pl.pallas_call(
        pick_kernel,
        out_shape=(shape((tokens + held_rows, width), bf16),) * 2,
        in_specs=[HBM] * 4,
        out_specs=(VMEM, VMEM),
        scratch_shapes=[pltpu.SemaphoreType.DMA((4,))],
        compiler_params=params(60),
        name="pick",
    )(*map(pin, sequences))
    swap = [(0, 1), (1, 0)]
    recv = lax.ppermute(send, "c", swap)

    factor = pl.pallas_call(
        decode_kernel,
        out_shape=shape((width, 2 * both), bf16),
        in_specs=[VMEM],
        out_specs=VMEM,
        compiler_params=params(16),
        cost_estimate=pl.CostEstimate(flops=COST, bytes_accessed=8 * width * both, transcendentals=0),
        name="decode",
    )(gathered.astype(jnp.float32))
    def products(*operands):
        return pl.pallas_call(
            product_kernel,
            out_shape=(shape((tokens, both)), shape((held_rows, both))),
            in_specs=[VMEM] * len(operands),
            out_specs=(VMEM, VMEM),
            compiler_params=params(16),
            name="products",
        )(*operands)

    other, held_other = products(factor, recv)
    own, held_own = products(factor, keep, held_other)
    pair = lax.all_gather(other, "c")

    to_plane, scale = pl.pallas_call(
        functools.partial(spread_kernel, share=share, copies=nx),
        out_shape=(shape((mates, 2 * share + rows, both), bf16), shape((8, both))),
        in_specs=[VMEM] * 4,
        out_specs=(VMEM, VMEM),
        compiler_params=params(40),
        name="spread",
    )(own, pair, held_own, held_other)
    features = pl.pallas_call(
        feature_kernel,
        out_shape=shape((2, half, half), bf16),
        in_specs=[VMEM] * 3,
        out_specs=VMEM,
        compiler_params=params(16),
        name="train_features",
    )(own, pair, scale)
    in_plane = lax.all_to_all(to_plane, PLANE, 0, 0)

    to_z = pl.pallas_call(
        functools.partial(normal_kernel, share=share),
        out_shape=shape((nz, rows, both), bf16),
        in_specs=[VMEM],
        out_specs=VMEM,
        scratch_shapes=[pltpu.VMEM((half, both), jnp.float32)],
        compiler_params=params(16),
        name="held_features",
    )(in_plane)
    held_every = lax.all_to_all(to_z, "z", 0, 0)

    partial = pl.pallas_call(
        functools.partial(influence_kernel, share=share, groups=ny),
        out_shape=shape((mates, 1, nz * nc * ny)),
        in_specs=[VMEM, VMEM],
        out_specs=VMEM,
        compiler_params=params(16),
        name="partial_influence",
    )(in_plane, held_every.reshape(nz * rows, both))
    back = lax.all_to_all(partial, PLANE, 0, 0)
    influence = jnp.sum(back, axis=(0, 1)).reshape(1, -1) * (1.0 / math.sqrt(half * both))
    return features.reshape(1, half * both), influence


def solution(mesh):
    ex, fsdp = mesh.devices.shape
    ny = nx = math.isqrt(fsdp)
    sizes = (ex // 2, 2, ny, nx)
    fine = Mesh(mesh.devices.reshape(sizes), ("z", "c", "y", "x"))
    e, f = ("z", "c"), ("y", "x")
    every = ("z", "c", "y", "x")
    placed = (
        P(every, None, None), P(every, None, None), P(e, f, None), P(e, f, None),
        P(f, None), P(None, f), P(), P(), P(f, None), P(f, None),
    )
    return jax.shard_map(
        functools.partial(shards, sizes=sizes),
        mesh=fine,
        in_specs=placed,
        out_specs=(P(every, None), P(every, None)),
        check_vma=False,
    )
```

```python
import functools
import math

import jax
import jax.numpy as jnp
from jax import lax
from jax.experimental import pallas as pl
from jax.experimental.pallas import tpu as pltpu
from jax.sharding import Mesh, PartitionSpec as P

EPSILON = 1e-06
HIGH = lax.Precision.HIGHEST
PLANE = ("y", "x", "c")
EXTRA = 8
LIFT = 14.0
COST = 20_000_000_000


def nt(a, b, precision=None):
    return lax.dot_general(
        a, b, (((1,), (1,)), ((), ())), precision=precision, preferred_element_type=jnp.float32
    )


def tn(a, b, precision=None):
    return lax.dot_general(
        a, b, (((0,), (0,)), ((), ())), precision=precision, preferred_element_type=jnp.float32
    )


def nn(a, b, precision=None):
    return lax.dot_general(
        a, b, (((1,), (0,)), ((), ())), precision=precision, preferred_element_type=jnp.float32
    )


def prepare_kernel(
    down_ref, up_ref, rank_down_ref, rank_up_ref, wide_up_ref, wide_down_ref,
    block_ref, adapter, rank, wide, sems,
):
    first = lax.axis_index("c") == 0

    def copies(of_adapter, of_rank, of_wide):
        return [
            pltpu.make_async_copy(of_adapter, adapter, sems.at[0]),
            pltpu.make_async_copy(of_rank, rank, sems.at[1]),
            pltpu.make_async_copy(of_wide, wide, sems.at[2]),
        ]

    of_g = copies(up_ref, rank_down_ref, wide_up_ref)
    of_x = copies(down_ref, rank_up_ref, wide_down_ref)

    @pl.when(first)
    def _():
        for one in of_g:
            one.start()

    @pl.when(jnp.logical_not(first))
    def _():
        for one in of_x:
            one.start()

    for one in of_g:
        one.wait()
    rows = adapter.shape[0]
    half = rank.shape[0]
    blank = jnp.zeros(rank.shape, rank.dtype)
    mine = rank[...]
    folded = nt(
        adapter[...],
        jnp.concatenate([jnp.where(first, blank, mine), jnp.where(first, mine, blank)], axis=0),
    )
    signs = wide[...].astype(jnp.float32)
    blank = jnp.zeros_like(signs)
    signs = jnp.concatenate([jnp.where(first, signs, blank), jnp.where(first, blank, signs)], axis=0)
    top = jnp.max(jnp.abs(folded), axis=0, keepdims=True)
    exponent = jnp.floor(jnp.log2(jnp.maximum(top, 2.0**-100)))
    lane = lax.broadcasted_iota(jnp.int32, (1, 2 * half), 1)
    is_folded = (lane >= half) == first
    exponent = jnp.where(is_folded, exponent, LIFT)
    block_ref[pl.ds(0, rows), :] = folded * jnp.exp2(LIFT - exponent) + signs.T
    block_ref[pl.ds(rows, EXTRA), :] = jnp.broadcast_to(exponent, (EXTRA, 2 * half))


def pick_kernel(xt_ref, gt_ref, xh_ref, gh_ref, keep_ref, send_ref, sems):
    first = lax.axis_index("c") == 0
    tokens = xt_ref.shape[0]
    held = xh_ref.shape[0]

    def copies(own_t, own_h, other_t, other_h):
        return [
            pltpu.make_async_copy(other_t, send_ref.at[pl.ds(0, tokens)], sems.at[0]),
            pltpu.make_async_copy(other_h, send_ref.at[pl.ds(tokens, held)], sems.at[1]),
            pltpu.make_async_copy(own_t, keep_ref.at[pl.ds(0, tokens)], sems.at[2]),
            pltpu.make_async_copy(own_h, keep_ref.at[pl.ds(tokens, held)], sems.at[3]),
        ]

    of_g = copies(gt_ref, gh_ref, xt_ref, xh_ref)
    of_x = copies(xt_ref, xh_ref, gt_ref, gh_ref)

    @pl.when(first)
    def _():
        for one in of_g:
            one.start()

    @pl.when(jnp.logical_not(first))
    def _():
        for one in of_x:
            one.start()

    for one in of_g:
        one.wait()


def decode_kernel(values_ref, factor_ref):
    chunks, tall, both = values_ref.shape
    local = tall - EXTRA
    for f in range(chunks):
        scale = jnp.exp2(values_ref[f, pl.ds(local, 1), :] - LIFT)
        value = values_ref[f, pl.ds(0, local), :] * scale
        high = value.astype(jnp.bfloat16)
        factor_ref[pl.ds(f * local, local), pl.ds(0, both)] = high
        low = value - high.astype(jnp.float32)
        factor_ref[pl.ds(f * local, local), pl.ds(both, both)] = low.astype(jnp.bfloat16)


def product_kernel(factor_ref, rows_ref, *refs):
    train_ref, held_ref = refs[-2:]
    tokens, both = train_ref.shape
    value = nn(rows_ref[...], factor_ref[...])
    value = value[:, :both] + value[:, both:]
    train_ref[...] = value[:tokens]
    held_ref[...] = value[tokens:]


def halves(value):
    high = value.astype(jnp.bfloat16)
    return high, (value - high.astype(jnp.float32)).astype(jnp.bfloat16)


def stacked(a, b):
    a_high, a_low = halves(a)
    b_high, b_low = halves(b)
    return tn(
        jnp.concatenate([a_high, a_high, a_low], axis=0),
        jnp.concatenate([b_high, b_low, b_high], axis=0),
    )


def joined(product, half):
    lane = lax.broadcasted_iota(jnp.int32, (half, 2 * half), 1)
    return jnp.where(lane < half, product[:half], product[half:])


def scale_of(values):
    return lax.rsqrt(jnp.sum(values * values, keepdims=True) * (1.0 / values.size) + EPSILON)


def kinds(own_ref, pair_ref):
    first = lax.axis_index("c") == 0
    own = own_ref[...]
    return jnp.where(first, own, pair_ref[0]), jnp.where(first, pair_ref[1], own)


def spread_kernel(
    own_ref, pair_ref, held_own_ref, held_other_ref, out_ref, features_ref, *, share, copies
):
    of_g, of_x = kinds(own_ref, pair_ref)
    product = stacked(of_x, of_g)
    half = product.shape[0] // 2
    values = joined(product, half)
    scale = scale_of(values)
    lane = lax.broadcasted_iota(jnp.int32, (half, 2 * half), 1)
    up = jnp.where(lane < half, product[:half] * scale, 0.0).astype(jnp.bfloat16)
    turned = stacked(of_g, of_x)
    down = jnp.where(lane < half, 0.0, turned[half:] * scale).astype(jnp.bfloat16)
    features_ref[...] = jnp.concatenate([paired(up, False), paired(down, True)], axis=0)
    rounded = (values * scale).astype(jnp.bfloat16)
    rows = half // copies
    groups = out_ref.shape[0] // (2 * copies)
    first = lax.axis_index("c") == 0
    own, other = held_own_ref[...], held_other_ref[...]
    for c, held in enumerate((jnp.where(first, own, other), jnp.where(first, other, own))):
        high = held.astype(jnp.bfloat16).astype(jnp.float32)
        low = held - high
        for v in range(groups):
            part = slice(v * share, (v + 1) * share)
            pair = jnp.concatenate([high[part], low[part]], axis=0).astype(jnp.bfloat16)
            for j in range(copies):
                i = (v * copies + j) * 2 + c
                out_ref[i, pl.ds(0, 2 * share), :] = pair
                out_ref[i, pl.ds(2 * share, rows), :] = rounded[j * rows : (j + 1) * rows]


def paired(values, at_right):
    rows, lanes = values.shape
    row = lax.broadcasted_iota(jnp.int32, (rows // 2, rows), 0)
    col = lax.broadcasted_iota(jnp.int32, (rows // 2, rows), 1)
    even = nn(jnp.where(col == 2 * row, 1.0, 0.0).astype(jnp.bfloat16), values)
    odd = nn(jnp.where(col == 2 * row + 1, 1.0, 0.0).astype(jnp.bfloat16), values)
    if at_right:
        return pltpu.roll(even, lanes // 2, 1) + odd
    return even + pltpu.roll(odd, lanes // 2, 1)


def normal_kernel(tokens_ref, out_ref, held_ref, *, share):
    count = tokens_ref.shape[0] // 2
    both = tokens_ref.shape[2]
    pairs = tokens_ref[:, pl.ds(0, 2 * share), :].astype(jnp.float32)
    tokens = (pairs[:, :share] + pairs[:, share:]).reshape(count, 2, share, both)
    of_g = tokens[:, 0].reshape(count * share, both)
    of_x = tokens[:, 1].reshape(count * share, both)
    product = stacked(of_x, of_g)
    half = both // 2
    values = joined(product, half)
    held_ref[...] = values * scale_of(values)
    rows = out_ref.shape[1]
    start = pl.multiple_of(lax.axis_index("x") * rows, rows)
    own = held_ref[pl.ds(start, rows), :].astype(jnp.bfloat16)
    for i in range(out_ref.shape[0]):
        out_ref[i] = own


def influence_kernel(tokens_ref, held_ref, out_ref, *, share, groups):
    slots = 2 * groups
    slot = lax.axis_index("c") * groups + lax.axis_index("y")
    mates, _, both = tokens_ref.shape
    rows = tokens_ref.shape[1] - 2 * share
    train = tokens_ref[:, pl.ds(2 * share, rows), :].reshape(mates * rows, both)
    every = nt(train, held_ref[...])
    n, m = every.shape
    r = lax.broadcasted_iota(jnp.int32, (n, m), 0)
    q = lax.broadcasted_iota(jnp.int32, (n, m), 1)
    every = jnp.where(lax.rem(r, rows) == lax.rem(q, rows), every, 0.0)
    trains = n // rows
    summed = jnp.sum(every.reshape(trains, rows, m), axis=1)
    row = lax.broadcasted_iota(jnp.int32, (m, out_ref.shape[2]), 0)
    col = lax.broadcasted_iota(jnp.int32, (m, out_ref.shape[2]), 1)
    place = jnp.where(col == lax.div(row, rows) * slots + slot, 1.0, 0.0)
    high = summed.astype(jnp.bfloat16).astype(jnp.float32)
    middle = (summed - high).astype(jnp.bfloat16).astype(jnp.float32)
    terms = jnp.concatenate([high, middle, summed - high - middle], axis=0)
    terms = nn(terms.astype(jnp.bfloat16), place.astype(jnp.bfloat16))
    placed = terms[:trains] + terms[trains : 2 * trains] + terms[2 * trains :]
    for i in range(trains):
        out_ref[i] = placed[i : i + 1]


def final_kernel(back_ref, flat_ref, features_ref, influence_ref, *, factor):
    total = back_ref[0]
    for i in range(1, back_ref.shape[0]):
        total += back_ref[i]
    influence_ref[...] = total * factor
    rows, lanes = flat_ref.shape
    flat = flat_ref[...].astype(jnp.bfloat16)
    for i in range(rows):
        features_ref[:, pl.ds(i * lanes, lanes)] = flat[i : i + 1]


VMEM = pl.BlockSpec(memory_space=pltpu.VMEM)
HBM = pl.BlockSpec(memory_space=pl.ANY)


def shape(dims, dtype=jnp.float32):
    return jax.ShapeDtypeStruct(dims, dtype)


def params(mib):
    return pltpu.CompilerParams(vmem_limit_bytes=mib << 20)


def shards(
    train_inputs, train_upstream, held_inputs, held_upstream, adapter_down, adapter_up,
    rank_signs_up, rank_signs_down, width_signs_up, width_signs_down, *, sizes,
):
    nz, nc, ny, nx = sizes
    mates = nc * ny * nx
    tokens, width = train_inputs.shape[1:]
    groups, share = held_inputs.shape[:2]
    held_rows = groups * share
    local, rank = adapter_down.shape
    half = rank_signs_up.shape[1]
    both = 2 * half
    rows = half // nx
    bf16 = jnp.bfloat16
    tall = local + EXTRA

    sequences = (
        train_inputs.reshape(tokens, width), train_upstream.reshape(tokens, width),
        held_inputs.reshape(held_rows, width), held_upstream.reshape(held_rows, width),
    )
    pin = lambda v: pltpu.with_memory_space_constraint(v, pltpu.HBM)
    block = pl.pallas_call(
        prepare_kernel,
        out_shape=shape((tall, both)),
        in_specs=[HBM] * 6,
        out_specs=VMEM,
        scratch_shapes=[
            pltpu.VMEM((local, rank), bf16),
            pltpu.VMEM((half, rank), bf16),
            pltpu.VMEM((half, local), bf16),
            pltpu.SemaphoreType.DMA((3,)),
        ],
        compiler_params=params(16),
        name="prepare",
    )(
        *map(pin, (
            adapter_down, adapter_up.T, rank_signs_down.T, rank_signs_up.T,
            width_signs_up.T, width_signs_down.T,
        ))
    )
    blocks = jnp.broadcast_to(block.astype(jnp.float16), (ny * nx, tall, both))
    gathered = lax.all_to_all(blocks, ("y", "x"), 0, 0)
    keep, send = pl.pallas_call(
        pick_kernel,
        out_shape=(shape((tokens + held_rows, width), bf16),) * 2,
        in_specs=[HBM] * 4,
        out_specs=(VMEM, VMEM),
        scratch_shapes=[pltpu.SemaphoreType.DMA((4,))],
        compiler_params=params(60),
        name="pick",
    )(*map(pin, sequences))
    swap = [(0, 1), (1, 0)]
    recv = lax.ppermute(send, "c", swap)

    factor = pl.pallas_call(
        decode_kernel,
        out_shape=shape((width, 2 * both), bf16),
        in_specs=[VMEM],
        out_specs=VMEM,
        compiler_params=params(16),
        cost_estimate=pl.CostEstimate(flops=COST, bytes_accessed=8 * width * both, transcendentals=0),
        name="decode",
    )(gathered.astype(jnp.float32))
    def products(*operands):
        return pl.pallas_call(
            product_kernel,
            out_shape=(shape((tokens, both)), shape((held_rows, both))),
            in_specs=[VMEM] * len(operands),
            out_specs=(VMEM, VMEM),
            compiler_params=params(16),
            name="products",
        )(*operands)

    other, held_other = products(factor, recv)
    own, held_own = products(factor, keep, held_other)
    pair = lax.all_gather(other, "c")

    to_plane, features = pl.pallas_call(
        functools.partial(spread_kernel, share=share, copies=nx),
        out_shape=(shape((mates, 2 * share + rows, both), bf16), shape((half, both))),
        in_specs=[VMEM] * 4,
        out_specs=(VMEM, VMEM),
        compiler_params=params(40),
        name="spread",
    )(own, pair, held_own, held_other)
    in_plane = lax.all_to_all(to_plane, PLANE, 0, 0)

    to_z = pl.pallas_call(
        functools.partial(normal_kernel, share=share),
        out_shape=shape((nz, rows, both), bf16),
        in_specs=[VMEM],
        out_specs=VMEM,
        scratch_shapes=[pltpu.VMEM((half, both), jnp.float32)],
        compiler_params=params(16),
        name="held_features",
    )(in_plane)
    held_every = lax.all_to_all(to_z, "z", 0, 0)

    partial = pl.pallas_call(
        functools.partial(influence_kernel, share=share, groups=ny),
        out_shape=shape((mates, 1, nz * nc * ny)),
        in_specs=[VMEM, VMEM],
        out_specs=VMEM,
        compiler_params=params(16),
        name="partial_influence",
    )(in_plane, held_every.reshape(nz * rows, both))
    back = lax.all_to_all(partial, PLANE, 0, 0)
    features, influence = pl.pallas_call(
        functools.partial(final_kernel, factor=1.0 / math.sqrt(half * both)),
        out_shape=(shape((1, half * both), bf16), shape((1, nz * nc * ny))),
        in_specs=[VMEM, VMEM],
        out_specs=(VMEM, VMEM),
        compiler_params=params(16),
        name="final",
    )(back, features)
    return features, influence


def solution(mesh):
    ex, fsdp = mesh.devices.shape
    ny = nx = math.isqrt(fsdp)
    sizes = (ex // 2, 2, ny, nx)
    fine = Mesh(mesh.devices.reshape(sizes), ("z", "c", "y", "x"))
    e, f = ("z", "c"), ("y", "x")
    every = ("z", "c", "y", "x")
    placed = (
        P(every, None, None), P(every, None, None), P(e, f, None), P(e, f, None),
        P(f, None), P(None, f), P(), P(), P(f, None), P(f, None),
    )
    return jax.shard_map(
        functools.partial(shards, sizes=sizes),
        mesh=fine,
        in_specs=placed,
        out_specs=(P(every, None), P(every, None)),
        check_vma=False,
    )
```

```python
import functools
import math

import jax
import jax.numpy as jnp
from jax import lax
from jax.experimental import pallas as pl
from jax.experimental.pallas import tpu as pltpu
from jax.sharding import Mesh, PartitionSpec as P

EPSILON = 1e-06
HIGH = lax.Precision.HIGHEST
PLANE = ("y", "x", "c")
EXTRA = 8
LIFT = 14.0
COST = 20_000_000_000


def nt(a, b, precision=None):
    return lax.dot_general(
        a, b, (((1,), (1,)), ((), ())), precision=precision, preferred_element_type=jnp.float32
    )


def tn(a, b, precision=None):
    return lax.dot_general(
        a, b, (((0,), (0,)), ((), ())), precision=precision, preferred_element_type=jnp.float32
    )


def nn(a, b, precision=None):
    return lax.dot_general(
        a, b, (((1,), (0,)), ((), ())), precision=precision, preferred_element_type=jnp.float32
    )


def prepare_kernel(
    down_ref, up_ref, rank_down_ref, rank_up_ref, wide_up_ref, wide_down_ref,
    block_ref, adapter, rank, wide, sems,
):
    first = lax.axis_index("c") == 0

    def copies(of_adapter, of_rank, of_wide):
        return [
            pltpu.make_async_copy(of_adapter, adapter, sems.at[0]),
            pltpu.make_async_copy(of_rank, rank, sems.at[1]),
            pltpu.make_async_copy(of_wide, wide, sems.at[2]),
        ]

    of_g = copies(up_ref, rank_down_ref, wide_up_ref)
    of_x = copies(down_ref, rank_up_ref, wide_down_ref)

    @pl.when(first)
    def _():
        for one in of_g:
            one.start()

    @pl.when(jnp.logical_not(first))
    def _():
        for one in of_x:
            one.start()

    for one in of_g:
        one.wait()
    rows = adapter.shape[0]
    half = rank.shape[0]
    blank = jnp.zeros(rank.shape, rank.dtype)
    mine = rank[...]
    folded = nt(
        adapter[...],
        jnp.concatenate([jnp.where(first, blank, mine), jnp.where(first, mine, blank)], axis=0),
    )
    signs = wide[...].astype(jnp.float32)
    blank = jnp.zeros_like(signs)
    signs = jnp.concatenate([jnp.where(first, signs, blank), jnp.where(first, blank, signs)], axis=0)
    top = jnp.max(jnp.abs(folded), axis=0, keepdims=True)
    exponent = jnp.floor(jnp.log2(jnp.maximum(top, 2.0**-100)))
    lane = lax.broadcasted_iota(jnp.int32, (1, 2 * half), 1)
    is_folded = (lane >= half) == first
    exponent = jnp.where(is_folded, exponent, LIFT)
    block_ref[pl.ds(0, rows), :] = folded * jnp.exp2(LIFT - exponent) + signs.T
    block_ref[pl.ds(rows, EXTRA), :] = jnp.broadcast_to(exponent, (EXTRA, 2 * half))


def pick_kernel(xt_ref, gt_ref, xh_ref, gh_ref, keep_ref, send_ref, sems):
    first = lax.axis_index("c") == 0
    tokens = xt_ref.shape[0]
    held = xh_ref.shape[0]

    def copies(own_t, own_h, other_t, other_h):
        return [
            pltpu.make_async_copy(other_t, send_ref.at[pl.ds(0, tokens)], sems.at[0]),
            pltpu.make_async_copy(other_h, send_ref.at[pl.ds(tokens, held)], sems.at[1]),
            pltpu.make_async_copy(own_t, keep_ref.at[pl.ds(0, tokens)], sems.at[2]),
            pltpu.make_async_copy(own_h, keep_ref.at[pl.ds(tokens, held)], sems.at[3]),
        ]

    of_g = copies(gt_ref, gh_ref, xt_ref, xh_ref)
    of_x = copies(xt_ref, xh_ref, gt_ref, gh_ref)

    @pl.when(first)
    def _():
        for one in of_g:
            one.start()

    @pl.when(jnp.logical_not(first))
    def _():
        for one in of_x:
            one.start()

    for one in of_g:
        one.wait()


def decode_kernel(values_ref, factor_ref, *, ny):
    chunks, tall, both = values_ref.shape
    local = tall - EXTRA
    for g in range(chunks):
        f = (g % ny) * (chunks // ny) + g // ny
        scale = jnp.exp2(values_ref[g, pl.ds(local, 1), :] - LIFT)
        value = values_ref[g, pl.ds(0, local), :] * scale
        high = value.astype(jnp.bfloat16)
        factor_ref[pl.ds(f * local, local), pl.ds(0, both)] = high
        low = value - high.astype(jnp.float32)
        factor_ref[pl.ds(f * local, local), pl.ds(both, both)] = low.astype(jnp.bfloat16)


def product_kernel(factor_ref, rows_ref, *refs):
    train_ref, held_ref = refs[-2:]
    tokens, both = train_ref.shape
    value = nn(rows_ref[...], factor_ref[...])
    value = value[:, :both] + value[:, both:]
    train_ref[...] = value[:tokens]
    held_ref[...] = value[tokens:]


def halves(value):
    high = value.astype(jnp.bfloat16)
    return high, (value - high.astype(jnp.float32)).astype(jnp.bfloat16)


def stacked(a, b):
    a_high, a_low = halves(a)
    b_high, b_low = halves(b)
    return tn(
        jnp.concatenate([a_high, a_high, a_low], axis=0),
        jnp.concatenate([b_high, b_low, b_high], axis=0),
    )


def joined(product, half):
    lane = lax.broadcasted_iota(jnp.int32, (half, 2 * half), 1)
    return jnp.where(lane < half, product[:half], product[half:])


def scale_of(values):
    return lax.rsqrt(jnp.sum(values * values, keepdims=True) * (1.0 / values.size) + EPSILON)


def kinds(own_ref, pair_ref):
    first = lax.axis_index("c") == 0
    own = own_ref[...]
    return jnp.where(first, own, pair_ref[0]), jnp.where(first, pair_ref[1], own)


def spread_kernel(
    own_ref, pair_ref, held_own_ref, held_other_ref, out_ref, features_ref, *, share, copies
):
    of_g, of_x = kinds(own_ref, pair_ref)
    product = stacked(of_x, of_g)
    half = product.shape[0] // 2
    values = joined(product, half)
    scale = scale_of(values)
    lane = lax.broadcasted_iota(jnp.int32, (half, 2 * half), 1)
    up = jnp.where(lane < half, product[:half] * scale, 0.0).astype(jnp.bfloat16)
    turned = product.T
    down = jnp.where(lane < half, 0.0, turned[half:] * scale).astype(jnp.bfloat16)
    features_ref[...] = jnp.concatenate([paired(up, False), paired(down, True)], axis=0)
    rounded = (values * scale).astype(jnp.bfloat16)
    rows = half // copies
    groups = out_ref.shape[0] // (2 * copies)
    first = lax.axis_index("c") == 0
    own, other = held_own_ref[...], held_other_ref[...]
    for c, held in enumerate((jnp.where(first, own, other), jnp.where(first, other, own))):
        high = held.astype(jnp.bfloat16).astype(jnp.float32)
        low = held - high
        for v in range(groups):
            part = slice(v * share, (v + 1) * share)
            pair = jnp.concatenate([high[part], low[part]], axis=0).astype(jnp.bfloat16)
            for j in range(copies):
                i = (v * copies + j) * 2 + c
                out_ref[i, pl.ds(0, 2 * share), :] = pair
                out_ref[i, pl.ds(2 * share, rows), :] = rounded[j * rows : (j + 1) * rows]


def paired(values, at_right):
    rows, lanes = values.shape
    row = lax.broadcasted_iota(jnp.int32, (rows // 2, rows), 0)
    col = lax.broadcasted_iota(jnp.int32, (rows // 2, rows), 1)
    even = nn(jnp.where(col == 2 * row, 1.0, 0.0).astype(jnp.bfloat16), values)
    odd = nn(jnp.where(col == 2 * row + 1, 1.0, 0.0).astype(jnp.bfloat16), values)
    if at_right:
        return pltpu.roll(even, lanes // 2, 1) + odd
    return even + pltpu.roll(odd, lanes // 2, 1)


def normal_kernel(tokens_ref, out_ref, held_ref, *, share):
    count = tokens_ref.shape[0] // 2
    both = tokens_ref.shape[2]
    pairs = tokens_ref[:, pl.ds(0, 2 * share), :].astype(jnp.float32)
    tokens = (pairs[:, :share] + pairs[:, share:]).reshape(count, 2, share, both)
    of_g = tokens[:, 0].reshape(count * share, both)
    of_x = tokens[:, 1].reshape(count * share, both)
    product = stacked(of_x, of_g)
    half = both // 2
    values = joined(product, half)
    held_ref[...] = values * scale_of(values)
    rows = out_ref.shape[1]
    start = pl.multiple_of(lax.axis_index("x") * rows, rows)
    own = held_ref[pl.ds(start, rows), :].astype(jnp.bfloat16)
    for i in range(out_ref.shape[0]):
        out_ref[i] = own


def influence_kernel(tokens_ref, held_ref, out_ref, *, share, groups):
    slots = 2 * groups
    slot = lax.axis_index("c") * groups + lax.axis_index("y")
    mates, _, both = tokens_ref.shape
    rows = tokens_ref.shape[1] - 2 * share
    train = tokens_ref[:, pl.ds(2 * share, rows), :].reshape(mates * rows, both)
    every = nt(train, held_ref[...])
    n, m = every.shape
    r = lax.broadcasted_iota(jnp.int32, (n, m), 0)
    q = lax.broadcasted_iota(jnp.int32, (n, m), 1)
    every = jnp.where(lax.rem(r, rows) == lax.rem(q, rows), every, 0.0)
    trains = n // rows
    summed = jnp.sum(every.reshape(trains, rows, m), axis=1)
    row = lax.broadcasted_iota(jnp.int32, (m, out_ref.shape[2]), 0)
    col = lax.broadcasted_iota(jnp.int32, (m, out_ref.shape[2]), 1)
    place = jnp.where(col == lax.div(row, rows) * slots + slot, 1.0, 0.0)
    high = summed.astype(jnp.bfloat16).astype(jnp.float32)
    middle = (summed - high).astype(jnp.bfloat16).astype(jnp.float32)
    terms = jnp.concatenate([high, middle, summed - high - middle], axis=0)
    terms = nn(terms.astype(jnp.bfloat16), place.astype(jnp.bfloat16))
    placed = terms[:trains] + terms[trains : 2 * trains] + terms[2 * trains :]
    for i in range(trains):
        out_ref[i] = placed[i : i + 1]


def final_kernel(back_ref, flat_ref, features_ref, influence_ref, *, factor):
    total = back_ref[0]
    for i in range(1, back_ref.shape[0]):
        total += back_ref[i]
    influence_ref[...] = total * factor
    rows, lanes = flat_ref.shape
    flat = flat_ref[...].astype(jnp.bfloat16)
    for i in range(rows):
        features_ref[:, pl.ds(i * lanes, lanes)] = flat[i : i + 1]


VMEM = pl.BlockSpec(memory_space=pltpu.VMEM)
HBM = pl.BlockSpec(memory_space=pl.ANY)


def shape(dims, dtype=jnp.float32):
    return jax.ShapeDtypeStruct(dims, dtype)


def params(mib):
    return pltpu.CompilerParams(vmem_limit_bytes=mib << 20)


def shards(
    train_inputs, train_upstream, held_inputs, held_upstream, adapter_down, adapter_up,
    rank_signs_up, rank_signs_down, width_signs_up, width_signs_down, *, sizes,
):
    nz, nc, ny, nx = sizes
    mates = nc * ny * nx
    tokens, width = train_inputs.shape[1:]
    groups, share = held_inputs.shape[:2]
    held_rows = groups * share
    local, rank = adapter_down.shape
    half = rank_signs_up.shape[1]
    both = 2 * half
    rows = half // nx
    bf16 = jnp.bfloat16
    tall = local + EXTRA

    sequences = (
        train_inputs.reshape(tokens, width), train_upstream.reshape(tokens, width),
        held_inputs.reshape(held_rows, width), held_upstream.reshape(held_rows, width),
    )
    pin = lambda v: pltpu.with_memory_space_constraint(v, pltpu.HBM)
    block = pl.pallas_call(
        prepare_kernel,
        out_shape=shape((tall, both)),
        in_specs=[HBM] * 6,
        out_specs=VMEM,
        scratch_shapes=[
            pltpu.VMEM((local, rank), bf16),
            pltpu.VMEM((half, rank), bf16),
            pltpu.VMEM((half, local), bf16),
            pltpu.SemaphoreType.DMA((3,)),
        ],
        compiler_params=params(16),
        name="prepare",
    )(
        *map(pin, (
            adapter_down, adapter_up.T, rank_signs_down.T, rank_signs_up.T,
            width_signs_up.T, width_signs_down.T,
        ))
    )
    blocks = jnp.broadcast_to(block.astype(jnp.float16), (ny * nx, tall, both))
    gathered = lax.all_to_all(blocks, ("x", "y"), 0, 0)
    keep, send = pl.pallas_call(
        pick_kernel,
        out_shape=(shape((tokens + held_rows, width), bf16),) * 2,
        in_specs=[HBM] * 4,
        out_specs=(VMEM, VMEM),
        scratch_shapes=[pltpu.SemaphoreType.DMA((4,))],
        compiler_params=params(60),
        name="pick",
    )(*map(pin, sequences))
    swap = [(0, 1), (1, 0)]
    recv = lax.ppermute(send, "c", swap)

    factor = pl.pallas_call(
        functools.partial(decode_kernel, ny=ny),
        out_shape=shape((width, 2 * both), bf16),
        in_specs=[VMEM],
        out_specs=VMEM,
        compiler_params=params(16),
        cost_estimate=pl.CostEstimate(flops=COST, bytes_accessed=8 * width * both, transcendentals=0),
        name="decode",
    )(gathered.astype(jnp.float32))
    def products(*operands):
        return pl.pallas_call(
            product_kernel,
            out_shape=(shape((tokens, both)), shape((held_rows, both))),
            in_specs=[VMEM] * len(operands),
            out_specs=(VMEM, VMEM),
            compiler_params=params(16),
            name="products",
        )(*operands)

    other, held_other = products(factor, recv)
    own, held_own = products(factor, keep, held_other)
    pair = lax.all_gather(other, "c")

    to_plane, features = pl.pallas_call(
        functools.partial(spread_kernel, share=share, copies=nx),
        out_shape=(shape((mates, 2 * share + rows, both), bf16), shape((half, both))),
        in_specs=[VMEM] * 4,
        out_specs=(VMEM, VMEM),
        compiler_params=params(40),
        name="spread",
    )(own, pair, held_own, held_other)
    in_plane = lax.all_to_all(to_plane, PLANE, 0, 0)

    to_z = pl.pallas_call(
        functools.partial(normal_kernel, share=share),
        out_shape=shape((nz, rows, both), bf16),
        in_specs=[VMEM],
        out_specs=VMEM,
        scratch_shapes=[pltpu.VMEM((half, both), jnp.float32)],
        compiler_params=params(16),
        name="held_features",
    )(in_plane)
    held_every = lax.all_to_all(to_z, "z", 0, 0)

    partial = pl.pallas_call(
        functools.partial(influence_kernel, share=share, groups=ny),
        out_shape=shape((mates, 1, nz * nc * ny)),
        in_specs=[VMEM, VMEM],
        out_specs=VMEM,
        compiler_params=params(16),
        name="partial_influence",
    )(in_plane, held_every.reshape(nz * rows, both))
    back = lax.all_to_all(partial, PLANE, 0, 0)
    features, influence = pl.pallas_call(
        functools.partial(final_kernel, factor=1.0 / math.sqrt(half * both)),
        out_shape=(shape((1, half * both), bf16), shape((1, nz * nc * ny))),
        in_specs=[VMEM, VMEM],
        out_specs=(VMEM, VMEM),
        compiler_params=params(16),
        name="final",
    )(back, features)
    return features, influence


def solution(mesh):
    ex, fsdp = mesh.devices.shape
    ny = nx = math.isqrt(fsdp)
    sizes = (ex // 2, 2, ny, nx)
    fine = Mesh(mesh.devices.reshape(sizes), ("z", "c", "y", "x"))
    e, f = ("z", "c"), ("y", "x")
    every = ("z", "c", "y", "x")
    placed = (
        P(every, None, None), P(every, None, None), P(e, f, None), P(e, f, None),
        P(f, None), P(None, f), P(), P(), P(f, None), P(f, None),
    )
    return jax.shard_map(
        functools.partial(shards, sizes=sizes),
        mesh=fine,
        in_specs=placed,
        out_specs=(P(every, None), P(every, None)),
        check_vma=False,
    )
```

```python
import functools
import math

import jax
import jax.numpy as jnp
from jax import lax
from jax.experimental import pallas as pl
from jax.experimental.pallas import tpu as pltpu
from jax.sharding import Mesh, PartitionSpec as P

EPSILON = 1e-06
HIGH = lax.Precision.HIGHEST
PLANE = ("y", "x", "c")
EXTRA = 8
LIFT = 14.0
COST = 20_000_000_000


def nt(a, b, precision=None):
    return lax.dot_general(
        a, b, (((1,), (1,)), ((), ())), precision=precision, preferred_element_type=jnp.float32
    )


def tn(a, b, precision=None):
    return lax.dot_general(
        a, b, (((0,), (0,)), ((), ())), precision=precision, preferred_element_type=jnp.float32
    )


def nn(a, b, precision=None):
    return lax.dot_general(
        a, b, (((1,), (0,)), ((), ())), precision=precision, preferred_element_type=jnp.float32
    )


def prepare_kernel(
    down_ref, up_ref, rank_down_ref, rank_up_ref, wide_up_ref, wide_down_ref,
    block_ref, adapter, rank, wide, sems,
):
    first = lax.axis_index("c") == 0

    def copies(of_adapter, of_rank, of_wide):
        return [
            pltpu.make_async_copy(of_adapter, adapter, sems.at[0]),
            pltpu.make_async_copy(of_rank, rank, sems.at[1]),
            pltpu.make_async_copy(of_wide, wide, sems.at[2]),
        ]

    of_g = copies(up_ref, rank_down_ref, wide_up_ref)
    of_x = copies(down_ref, rank_up_ref, wide_down_ref)

    @pl.when(first)
    def _():
        for one in of_g:
            one.start()

    @pl.when(jnp.logical_not(first))
    def _():
        for one in of_x:
            one.start()

    for one in of_g:
        one.wait()
    rows = adapter.shape[0]
    half = rank.shape[0]
    blank = jnp.zeros(rank.shape, rank.dtype)
    mine = rank[...]
    folded = nt(
        adapter[...],
        jnp.concatenate([blank, mine], axis=0),
    )
    signs = wide[...].astype(jnp.float32)
    blank = jnp.zeros_like(signs)
    signs = jnp.concatenate([signs, blank], axis=0)
    top = jnp.max(jnp.abs(folded), axis=0, keepdims=True)
    exponent = jnp.floor(jnp.log2(jnp.maximum(top, 2.0**-100)))
    lane = lax.broadcasted_iota(jnp.int32, (1, 2 * half), 1)
    exponent = jnp.where(lane >= half, exponent, LIFT)
    block_ref[pl.ds(0, rows), :] = folded * jnp.exp2(LIFT - exponent) + signs.T
    block_ref[pl.ds(rows, EXTRA), :] = jnp.broadcast_to(exponent, (EXTRA, 2 * half))


def pick_kernel(xt_ref, gt_ref, xh_ref, gh_ref, keep_ref, send_ref, sems):
    first = lax.axis_index("c") == 0
    tokens = xt_ref.shape[0]
    held = xh_ref.shape[0]

    def copies(own_t, own_h, other_t, other_h):
        return [
            pltpu.make_async_copy(other_t, send_ref.at[pl.ds(0, tokens)], sems.at[0]),
            pltpu.make_async_copy(other_h, send_ref.at[pl.ds(tokens, held)], sems.at[1]),
            pltpu.make_async_copy(own_t, keep_ref.at[pl.ds(0, tokens)], sems.at[2]),
            pltpu.make_async_copy(own_h, keep_ref.at[pl.ds(tokens, held)], sems.at[3]),
        ]

    of_g = copies(gt_ref, gh_ref, xt_ref, xh_ref)
    of_x = copies(xt_ref, xh_ref, gt_ref, gh_ref)

    @pl.when(first)
    def _():
        for one in of_g:
            one.start()

    @pl.when(jnp.logical_not(first))
    def _():
        for one in of_x:
            one.start()

    for one in of_g:
        one.wait()


def decode_kernel(values_ref, factor_ref):
    chunks, tall, both = values_ref.shape
    local = tall - EXTRA
    for f in range(chunks):
        scale = jnp.exp2(values_ref[f, pl.ds(local, 1), :] - LIFT)
        value = values_ref[f, pl.ds(0, local), :] * scale
        high = value.astype(jnp.bfloat16)
        factor_ref[pl.ds(f * local, local), pl.ds(0, both)] = high
        low = value - high.astype(jnp.float32)
        factor_ref[pl.ds(f * local, local), pl.ds(both, both)] = low.astype(jnp.bfloat16)


def product_kernel(factor_ref, rows_ref, *refs):
    train_ref, held_ref = refs[-2:]
    tokens, both = train_ref.shape
    value = nn(rows_ref[...], factor_ref[...])
    value = value[:, :both] + value[:, both:]
    train_ref[...] = value[:tokens]
    held_ref[...] = value[tokens:]


def halves(value):
    high = value.astype(jnp.bfloat16)
    return high, (value - high.astype(jnp.float32)).astype(jnp.bfloat16)


def stacked(a, b):
    a_high, a_low = halves(a)
    b_high, b_low = halves(b)
    return tn(
        jnp.concatenate([a_high, a_high, a_low], axis=0),
        jnp.concatenate([b_high, b_low, b_high], axis=0),
    )


def joined(product, half):
    lane = lax.broadcasted_iota(jnp.int32, (half, 2 * half), 1)
    return jnp.where(lane < half, product[half:], product[:half])


def scale_of(values):
    return lax.rsqrt(jnp.sum(values * values, keepdims=True) * (1.0 / values.size) + EPSILON)


def kinds(own_ref, pair_ref):
    first = lax.axis_index("c") == 0
    own = own_ref[...]
    return jnp.where(first, own, pair_ref[0]), jnp.where(first, pair_ref[1], own)


def spread_kernel(
    own_ref, pair_ref, held_own_ref, held_other_ref, out_ref, features_ref, *, share, copies
):
    of_g, of_x = kinds(own_ref, pair_ref)
    product = stacked(of_x, of_g)
    half = product.shape[0] // 2
    values = joined(product, half)
    scale = scale_of(values)
    lane = lax.broadcasted_iota(jnp.int32, (half, 2 * half), 1)
    up = jnp.where(lane < half, product[half:] * scale, 0.0).astype(jnp.bfloat16)
    turned = stacked(of_g, of_x)
    down = jnp.where(lane < half, turned[half:] * scale, 0.0).astype(jnp.bfloat16)
    features_ref[...] = jnp.concatenate([paired(up, False), paired(down, False)], axis=0)
    rounded = (values * scale).astype(jnp.bfloat16)
    rows = half // copies
    groups = out_ref.shape[0] // (2 * copies)
    first = lax.axis_index("c") == 0
    own, other = held_own_ref[...], held_other_ref[...]
    for c, held in enumerate((jnp.where(first, own, other), jnp.where(first, other, own))):
        high = held.astype(jnp.bfloat16).astype(jnp.float32)
        low = held - high
        for v in range(groups):
            part = slice(v * share, (v + 1) * share)
            pair = jnp.concatenate([high[part], low[part]], axis=0).astype(jnp.bfloat16)
            for j in range(copies):
                i = (v * copies + j) * 2 + c
                out_ref[i, pl.ds(0, 2 * share), :] = pair
                out_ref[i, pl.ds(2 * share, rows), :] = rounded[j * rows : (j + 1) * rows]


def paired(values, at_right):
    rows, lanes = values.shape
    row = lax.broadcasted_iota(jnp.int32, (rows // 2, rows), 0)
    col = lax.broadcasted_iota(jnp.int32, (rows // 2, rows), 1)
    even = nn(jnp.where(col == 2 * row, 1.0, 0.0).astype(jnp.bfloat16), values)
    odd = nn(jnp.where(col == 2 * row + 1, 1.0, 0.0).astype(jnp.bfloat16), values)
    if at_right:
        return pltpu.roll(even, lanes // 2, 1) + odd
    return even + pltpu.roll(odd, lanes // 2, 1)


def normal_kernel(tokens_ref, out_ref, held_ref, *, share):
    count = tokens_ref.shape[0] // 2
    both = tokens_ref.shape[2]
    pairs = tokens_ref[:, pl.ds(0, 2 * share), :].astype(jnp.float32)
    tokens = (pairs[:, :share] + pairs[:, share:]).reshape(count, 2, share, both)
    of_g = tokens[:, 0].reshape(count * share, both)
    of_x = tokens[:, 1].reshape(count * share, both)
    product = stacked(of_x, of_g)
    half = both // 2
    values = joined(product, half)
    held_ref[...] = values * scale_of(values)
    rows = out_ref.shape[1]
    start = pl.multiple_of(lax.axis_index("x") * rows, rows)
    own = held_ref[pl.ds(start, rows), :].astype(jnp.bfloat16)
    for i in range(out_ref.shape[0]):
        out_ref[i] = own


def influence_kernel(tokens_ref, held_ref, out_ref, *, share, groups):
    slots = 2 * groups
    slot = lax.axis_index("c") * groups + lax.axis_index("y")
    mates, _, both = tokens_ref.shape
    rows = tokens_ref.shape[1] - 2 * share
    train = tokens_ref[:, pl.ds(2 * share, rows), :].reshape(mates * rows, both)
    every = nt(train, held_ref[...])
    n, m = every.shape
    r = lax.broadcasted_iota(jnp.int32, (n, m), 0)
    q = lax.broadcasted_iota(jnp.int32, (n, m), 1)
    every = jnp.where(lax.rem(r, rows) == lax.rem(q, rows), every, 0.0)
    trains = n // rows
    summed = jnp.sum(every.reshape(trains, rows, m), axis=1)
    row = lax.broadcasted_iota(jnp.int32, (m, out_ref.shape[2]), 0)
    col = lax.broadcasted_iota(jnp.int32, (m, out_ref.shape[2]), 1)
    place = jnp.where(col == lax.div(row, rows) * slots + slot, 1.0, 0.0)
    high = summed.astype(jnp.bfloat16).astype(jnp.float32)
    middle = (summed - high).astype(jnp.bfloat16).astype(jnp.float32)
    terms = jnp.concatenate([high, middle, summed - high - middle], axis=0)
    terms = nn(terms.astype(jnp.bfloat16), place.astype(jnp.bfloat16))
    placed = terms[:trains] + terms[trains : 2 * trains] + terms[2 * trains :]
    for i in range(trains):
        out_ref[i] = placed[i : i + 1]


def final_kernel(back_ref, flat_ref, features_ref, influence_ref, *, factor):
    total = back_ref[0]
    for i in range(1, back_ref.shape[0]):
        total += back_ref[i]
    influence_ref[...] = total * factor
    rows, lanes = flat_ref.shape
    flat = flat_ref[...].astype(jnp.bfloat16)
    for i in range(rows):
        features_ref[:, pl.ds(i * lanes, lanes)] = flat[i : i + 1]


VMEM = pl.BlockSpec(memory_space=pltpu.VMEM)
HBM = pl.BlockSpec(memory_space=pl.ANY)


def shape(dims, dtype=jnp.float32):
    return jax.ShapeDtypeStruct(dims, dtype)


def params(mib):
    return pltpu.CompilerParams(vmem_limit_bytes=mib << 20)


def shards(
    train_inputs, train_upstream, held_inputs, held_upstream, adapter_down, adapter_up,
    rank_signs_up, rank_signs_down, width_signs_up, width_signs_down, *, sizes,
):
    nz, nc, ny, nx = sizes
    mates = nc * ny * nx
    tokens, width = train_inputs.shape[1:]
    groups, share = held_inputs.shape[:2]
    held_rows = groups * share
    local, rank = adapter_down.shape
    half = rank_signs_up.shape[1]
    both = 2 * half
    rows = half // nx
    bf16 = jnp.bfloat16
    tall = local + EXTRA

    sequences = (
        train_inputs.reshape(tokens, width), train_upstream.reshape(tokens, width),
        held_inputs.reshape(held_rows, width), held_upstream.reshape(held_rows, width),
    )
    pin = lambda v: pltpu.with_memory_space_constraint(v, pltpu.HBM)
    block = pl.pallas_call(
        prepare_kernel,
        out_shape=shape((tall, both)),
        in_specs=[HBM] * 6,
        out_specs=VMEM,
        scratch_shapes=[
            pltpu.VMEM((local, rank), bf16),
            pltpu.VMEM((half, rank), bf16),
            pltpu.VMEM((half, local), bf16),
            pltpu.SemaphoreType.DMA((3,)),
        ],
        compiler_params=params(16),
        name="prepare",
    )(
        *map(pin, (
            adapter_down, adapter_up.T, rank_signs_down.T, rank_signs_up.T,
            width_signs_up.T, width_signs_down.T,
        ))
    )
    blocks = jnp.broadcast_to(block.astype(jnp.float16), (ny * nx, tall, both))
    gathered = lax.all_to_all(blocks, ("y", "x"), 0, 0)
    keep, send = pl.pallas_call(
        pick_kernel,
        out_shape=(shape((tokens + held_rows, width), bf16),) * 2,
        in_specs=[HBM] * 4,
        out_specs=(VMEM, VMEM),
        scratch_shapes=[pltpu.SemaphoreType.DMA((4,))],
        compiler_params=params(60),
        name="pick",
    )(*map(pin, sequences))
    swap = [(0, 1), (1, 0)]
    recv = lax.ppermute(send, "c", swap)

    factor = pl.pallas_call(
        decode_kernel,
        out_shape=shape((width, 2 * both), bf16),
        in_specs=[VMEM],
        out_specs=VMEM,
        compiler_params=params(16),
        cost_estimate=pl.CostEstimate(flops=COST, bytes_accessed=8 * width * both, transcendentals=0),
        name="decode",
    )(gathered.astype(jnp.float32))
    def products(*operands):
        return pl.pallas_call(
            product_kernel,
            out_shape=(shape((tokens, both)), shape((held_rows, both))),
            in_specs=[VMEM] * len(operands),
            out_specs=(VMEM, VMEM),
            compiler_params=params(16),
            name="products",
        )(*operands)

    other, held_other = products(factor, recv)
    own, held_own = products(factor, keep, held_other)
    pair = lax.all_gather(other, "c")

    to_plane, features = pl.pallas_call(
        functools.partial(spread_kernel, share=share, copies=nx),
        out_shape=(shape((mates, 2 * share + rows, both), bf16), shape((half, both))),
        in_specs=[VMEM] * 4,
        out_specs=(VMEM, VMEM),
        compiler_params=params(40),
        name="spread",
    )(own, pair, held_own, held_other)
    in_plane = lax.all_to_all(to_plane, PLANE, 0, 0)

    to_z = pl.pallas_call(
        functools.partial(normal_kernel, share=share),
        out_shape=shape((nz, rows, both), bf16),
        in_specs=[VMEM],
        out_specs=VMEM,
        scratch_shapes=[pltpu.VMEM((half, both), jnp.float32)],
        compiler_params=params(16),
        name="held_features",
    )(in_plane)
    held_every = lax.all_to_all(to_z, "z", 0, 0)

    partial = pl.pallas_call(
        functools.partial(influence_kernel, share=share, groups=ny),
        out_shape=shape((mates, 1, nz * nc * ny)),
        in_specs=[VMEM, VMEM],
        out_specs=VMEM,
        compiler_params=params(16),
        name="partial_influence",
    )(in_plane, held_every.reshape(nz * rows, both))
    back = lax.all_to_all(partial, PLANE, 0, 0)
    features, influence = pl.pallas_call(
        functools.partial(final_kernel, factor=1.0 / math.sqrt(half * both)),
        out_shape=(shape((1, half * both), bf16), shape((1, nz * nc * ny))),
        in_specs=[VMEM, VMEM],
        out_specs=(VMEM, VMEM),
        compiler_params=params(16),
        name="final",
    )(back, features)
    return features, influence


def solution(mesh):
    ex, fsdp = mesh.devices.shape
    ny = nx = math.isqrt(fsdp)
    sizes = (ex // 2, 2, ny, nx)
    fine = Mesh(mesh.devices.reshape(sizes), ("z", "c", "y", "x"))
    e, f = ("z", "c"), ("y", "x")
    every = ("z", "c", "y", "x")
    placed = (
        P(every, None, None), P(every, None, None), P(e, f, None), P(e, f, None),
        P(f, None), P(None, f), P(), P(), P(f, None), P(f, None),
    )
    return jax.shard_map(
        functools.partial(shards, sizes=sizes),
        mesh=fine,
        in_specs=placed,
        out_specs=(P(every, None), P(every, None)),
        check_vma=False,
    )
```
